512 devices in a mesh: chain: 128 (over z, y, core), rep: 4 (over x).
Axes of the slice: x: 4, y: 4, z: 16, core: 2. Of those that a mesh axis runs over, the one named last changes fastest.
Arguments:
- sub_inverse: bfloat16 [128, 4, 384, 384], P('chain', 'rep'), may hold values from -1.5 to 1.5
- sub_rhs: bfloat16 [128, 4, 384, 256], P('chain', 'rep'), may hold values from -6 to 6
- sub_tiles: int32 [128, 4], P('chain', 'rep'), may hold values from 1 to 3, as said below
- update: bfloat16 [128, 4, 768, 384], P('chain', 'rep'), may hold values from -0.3125 to 0.3125
- update_rows: int32 [128, 4, 6], P('chain', 'rep'), may hold values from 0 to 1
- level_inverse: float32 [128, 256, 256], P('chain'), may hold values from -1.5 to 1.5
- coupling: float32 [128, 256, 128], P('chain'), may hold values from -1.5 to 1.5
- level_rhs: float32 [128, 256, 256], P('chain'), may hold values from -6 to 6
Outputs:
- level_solution: float32 [128, 256, 256], P('chain')
- sub_solution: float32 [128, 4, 384, 256], P('chain', 'rep')
The draws below stay inside these ranges and needn't reach their ends.
Inputs may be any that keep to these rules, and one draw needn't show every extreme that they name: `sub_tiles`: some subtree block has all 3 tiles live.
All inputs are finite; a program needn't handle non-finite values.
Results may differ from the reference program's by a relative error of at most 0.0049.
Values sent between devices are 32-bit elements; how exact they have to be, the bound alone decides.
No kernel may reach another device: no remote copies, remote signals or barrier semaphores. Data moves between devices by JAX's collectives and lax.ppermute only.
A program may use at most 128 MiB of HBM per device.

```python
import math
import jax
import jax.numpy as jnp
from jax import lax

TILE = 128
RHS = 256
TILES = 2
SUBT = 3
UT = 6
W = 256
SUB = 384
SUPERNODE_LEVELS = 128
REPS = 4


def draw_sub_inverse(key, part):
    key = jax.random.fold_in(key, 37)
    first, second = jax.random.split(key)
    diag_part = jax.random.uniform(first, (SUPERNODE_LEVELS, REPS, SUB), minval=0.8, maxval=1.2)
    off = jnp.clip(jax.random.normal(second, (SUPERNODE_LEVELS, REPS, SUB, SUB)), -4.0, 4.0)
    rows = jax.lax.broadcasted_iota(jnp.int32, (SUB, SUB), 0)
    cols = jax.lax.broadcasted_iota(jnp.int32, (SUB, SUB), 1)
    lower = jnp.where(rows > cols, off * (0.5 / math.sqrt(SUB)), 0.0)
    eye = jnp.eye(SUB, dtype=jnp.float32)
    return (lower + eye * diag_part[..., :, None]).astype(jnp.bfloat16)


def draw_sub_tiles(key, part):
    key = jax.random.fold_in(key, 41)
    first, second = jax.random.split(key)
    counts = jax.random.randint(first, (SUPERNODE_LEVELS * REPS,), 1, SUBT + 1)
    spot = jax.random.randint(second, (), 0, SUPERNODE_LEVELS * REPS)
    counts = jnp.where(jnp.arange(SUPERNODE_LEVELS * REPS) == spot, SUBT, counts)
    return counts.reshape(SUPERNODE_LEVELS, REPS).astype(jnp.int32)


def draw_level_inverse(key, part):
    key = jax.random.fold_in(key, 11)
    first, second = jax.random.split(key)
    diag_part = jax.random.uniform(first, (SUPERNODE_LEVELS, W), minval=0.98, maxval=1.0)
    off = jnp.clip(jax.random.normal(second, (SUPERNODE_LEVELS, W, W)), -4.0, 4.0)
    eye = jnp.eye(W, dtype=jnp.float32)
    return eye * diag_part[:, :, None] + (1.0 - eye) * off * (0.1 / math.sqrt(W))


def draw_coupling(key, part):
    key = jax.random.fold_in(key, 23)
    first, second, third_member, fourth, fifth = jax.random.split(key, 5)
    share = 0.5
    off = jnp.clip(jax.random.normal(fifth, (SUPERNODE_LEVELS, W, TILE)), -4.0, 4.0)
    slow = jax.random.uniform(first, (1, TILE)) < share
    fast_rate = jnp.exp(jax.random.uniform(second, (SUPERNODE_LEVELS, TILE), minval=math.log(0.3), maxval=math.log(0.9)))
    slow_rate = jnp.full((SUPERNODE_LEVELS, TILE), 0.5 ** (1.0 / SUPERNODE_LEVELS), jnp.float32)
    decay_rate = jnp.where(slow, slow_rate, fast_rate)
    sudden_spike = jax.random.uniform(third_member, (SUPERNODE_LEVELS, 1)) < 0.05
    objective_loss = jax.random.uniform(fourth, (SUPERNODE_LEVELS, 1), minval=0.5, maxval=0.8)
    decay_rate = jnp.where(sudden_spike, decay_rate * objective_loss, decay_rate)
    rows = jax.lax.broadcasted_iota(jnp.int32, (W, TILE), 0)
    cols = jax.lax.broadcasted_iota(jnp.int32, (W, TILE), 1)
    diag = (rows == cols + (W - TILE)).astype(jnp.float32)
    return -(diag * decay_rate[:, None, :] + (1.0 - diag) * off * (0.1 / math.sqrt(TILE)))


def plant(result, own_key, least, high):
    place = [jax.random.randint(jax.random.fold_in(own_key, axis), (), 0, length) for axis, length in enumerate(result.shape)]
    longest = result.shape.index(max(result.shape))
    next_to = place[:longest] + [(place[longest] + 1) % result.shape[longest]] + place[longest + 1:]
    return result.at[tuple(place)].set(least).at[tuple(next_to)].set(high)


def steps_of(own_key, dims, cuts, least, high):
    def one(axis_at, blocks):
        heights = jax.random.uniform(jax.random.fold_in(jax.random.fold_in(own_key, 6), axis_at), (blocks,), jnp.float32, least / len(cuts), high / len(cuts))
        return jnp.repeat(jnp.exp(heights), dims[axis_at] // blocks).reshape((-1,) + (1,) * (len(dims) - axis_at - 1))

    loudness = one(*cuts[0])
    for cut in cuts[1:]:
        loudness = loudness * one(*cut)
    return loudness


def noise(rng, dims, deviation, bound, cuts=(), kind=jnp.bfloat16):
    values = jax.random.normal(rng, dims, jnp.float32) * deviation
    if len(cuts) > 0:
        values = steps_of(rng, dims, cuts, -0.22, 0.18) * values
    return jnp.clip(values, min=-bound, max=bound).astype(kind)


def setup_inputs(seed: int = 0) -> dict:
    key_list = jax.random.split(jax.random.key(seed), 9)
    sub_inverse = draw_sub_inverse(jax.random.fold_in(key_list[8], 71), 0)
    sub_rhs = noise(key_list[1], (SUPERNODE_LEVELS, REPS, SUB, RHS), 1.0, 6.0, ((0, 128), (1, 4)))
    sub_tiles = draw_sub_tiles(jax.random.fold_in(key_list[8], 71), 0)
    update = noise(key_list[3], (SUPERNODE_LEVELS, REPS, UT * TILE, SUB), SUB ** -0.5, 0.3125, ((0, 128), (1, 4)))
    update_rows = plant(jax.random.randint(key_list[4], (SUPERNODE_LEVELS, REPS, UT), 0, TILES), jax.random.fold_in(key_list[4], 1), 0, TILES - 1).astype(jnp.int32)
    level_inverse = draw_level_inverse(jax.random.fold_in(key_list[8], 71), 0)
    coupling = draw_coupling(jax.random.fold_in(key_list[8], 71), 0)
    level_rhs = noise(key_list[7], (SUPERNODE_LEVELS, W, RHS), 1.0, 6.0, ((0, 128),), jnp.float32)
    return {"sub_inverse": sub_inverse, "sub_rhs": sub_rhs, "sub_tiles": sub_tiles, "update": update, "update_rows": update_rows, "level_inverse": level_inverse, "coupling": coupling, "level_rhs": level_rhs}


def live_rows(count):
    return lax.broadcasted_iota(jnp.int32, (SUB, 1), 0) < TILE * count


def placement_table(rows_of_update):
    return (rows_of_update[None, :] == lax.broadcasted_iota(jnp.int32, (TILES, UT), 0)).astype(jnp.float32)


def level_forward(pieces):
    subtree_inverse, rhs_sub, counts, block, rows_of_update = pieces
    total = jnp.zeros((W, RHS), jnp.float32)
    forwards = []
    for member in range(REPS):
        live = live_rows(counts[member])
        masked = jnp.where(live, rhs_sub[member], jnp.zeros_like(rhs_sub[member]))
        solved = jnp.dot(subtree_inverse[member], masked, preferred_element_type=jnp.float32)
        forward_sub = jnp.where(live, solved, jnp.zeros_like(solved)).astype(jnp.bfloat16)
        contrib = jnp.dot(block[member], forward_sub, preferred_element_type=jnp.float32)
        table = placement_table(rows_of_update[member])
        placed = jnp.einsum("st,tpr->spr", table, contrib.reshape(UT, TILE, RHS), precision=lax.Precision.HIGHEST)
        total = total + placed.reshape(W, RHS)
        forwards.append(forward_sub)
    return jnp.stack(forwards), total


def level_backward(pieces):
    subtree_inverse, counts, block, rows_of_update, forward_sub, solution = pieces
    rounded = lax.optimization_barrier(solution.astype(jnp.bfloat16)).astype(jnp.float32)
    results = []
    for member in range(REPS):
        table = placement_table(rows_of_update[member])
        picked = jnp.einsum("st,spr->tpr", table, rounded.reshape(TILES, TILE, RHS), precision=lax.Precision.HIGHEST)
        picked = picked.reshape(UT * TILE, RHS).astype(jnp.bfloat16)
        pulled = jnp.dot(block[member].T, picked, preferred_element_type=jnp.float32)
        live = live_rows(counts[member])
        leftover_remainder = (forward_sub[member].astype(jnp.float32) - jnp.where(live, pulled, jnp.zeros_like(pulled))).astype(jnp.bfloat16)
        final = jnp.dot(subtree_inverse[member].T, leftover_remainder, preferred_element_type=jnp.float32)
        results.append(jnp.where(live, final, jnp.zeros_like(final)))
    return jnp.stack(results)


def reference(sub_inverse, sub_rhs, sub_tiles, update, update_rows, level_inverse, coupling, level_rhs):
    highest = lax.Precision.HIGHEST
    forward_subs, totals = lax.map(level_forward, (sub_inverse, sub_rhs, sub_tiles, update, update_rows))

    def forward_step(previous, pieces):
        inverse, couple, rhs, total = pieces
        pulled = jnp.dot(couple, previous[W - TILE:], precision=highest)
        current = jnp.dot(inverse, rhs - total - pulled, precision=highest)
        return current, current

    start = jnp.zeros((W, RHS), jnp.float32)
    _, forward = lax.scan(forward_step, start, (level_inverse, coupling, level_rhs, totals))
    later_coupling = jnp.concatenate([coupling[1:], jnp.zeros_like(coupling[:1])], axis=0)

    def backward_step(following, pieces):
        inverse, couple_next, forward_level = pieces
        pushed = jnp.dot(couple_next.T, following, precision=highest)
        placed = jnp.concatenate([jnp.zeros((W - TILE, RHS), jnp.float32), pushed], axis=0)
        current = jnp.dot(inverse.T, forward_level - placed, precision=highest)
        return current, current

    _, level_solution = lax.scan(backward_step, start, (level_inverse, later_coupling, forward), reverse=True)
    sub_solution = lax.map(level_backward, (sub_inverse, sub_tiles, update, update_rows, forward_subs, level_solution))
    return level_solution, sub_solution
```

```python
import functools

import jax
import jax.numpy as jnp
from jax import lax
from jax.experimental import pallas as pl
from jax.experimental.pallas import tpu as pltpu
from jax.sharding import PartitionSpec as P

TILE = 128
HIGHEST = lax.Precision.HIGHEST
SWAP = (1, 2, 6, 8, 16, 32, 96)


def dot(a, b, dims=((1,), (0,)), precision=HIGHEST):
    return lax.dot_general(
        a, b, (dims, ((), ())), precision=precision, preferred_element_type=jnp.float32
    )


def swap(value, j, count):
    return lax.ppermute(value, "chain", [(k, k ^ SWAP[j]) for k in range(count)])


def level_maps(inverse, couple):
    gain = -dot(inverse, couple)
    return gain, jnp.concatenate([gain[TILE:], -dot(gain, gain, ((0,), (0,)))], axis=0)


def subtree_forward(subtree_inverse, rhs_sub, live, block, rows, rhs_level, inverse):
    masked = jnp.where(live, rhs_sub, jnp.zeros_like(rhs_sub))
    solved = jnp.dot(subtree_inverse, masked, preferred_element_type=jnp.float32)
    forward_sub = jnp.where(live, solved, jnp.zeros_like(solved)).astype(jnp.bfloat16)
    contrib = jnp.dot(block, forward_sub, preferred_element_type=jnp.float32)
    contrib = contrib.reshape(rows.shape[0], TILE, -1)
    tiles = inverse.shape[0] // TILE
    placed = [
        sum(jnp.where(rows[t] == s, contrib[t], 0.0) for t in range(rows.shape[0]))
        for s in range(tiles)
    ]
    rest = 0.25 * rhs_level - jnp.concatenate(placed, axis=0)
    return forward_sub, dot(rest, inverse, ((0,), (1,)))


def subtree_backward(solution, forward_sub, subtree_inverse, live, block, rows):
    rounded = solution.astype(jnp.bfloat16)
    picked = jnp.concatenate(
        [
            jnp.where(rows[t] == 0, rounded[:TILE], rounded[TILE:])
            for t in range(rows.shape[0])
        ],
        axis=0,
    )
    pulled = dot(block, picked, ((0,), (0,)), None)
    residue = (forward_sub.astype(jnp.float32) - jnp.where(live, pulled, 0.0)).astype(
        jnp.bfloat16
    )
    final = dot(subtree_inverse, residue, ((0,), (0,)), None)
    return jnp.where(live, final, 0.0)


def shards(
    sub_inverse, sub_rhs, sub_tiles, update, update_rows, level_inverse, coupling, level_rhs
):
    count, reps = lax.axis_size("chain"), lax.axis_size("rep")
    place = lax.axis_index("chain")
    subtree_inverse, block, rows = sub_inverse[0, 0], update[0, 0], update_rows[0, 0]
    inverse, couple = level_inverse[0], coupling[0]
    sub_rows = subtree_inverse.shape[0]
    live = lax.broadcasted_iota(jnp.int32, (sub_rows, 1), 0) < TILE * sub_tiles[0, 0]
    gain, maps = level_maps(inverse, couple)
    forward_sub, part = subtree_forward(
        subtree_inverse, sub_rhs[0, 0], live, block, rows, level_rhs[0], inverse
    )
    columns = part.shape[0] // reps
    parts = lax.all_to_all(part.reshape(reps, columns, -1), "rep", 0, 0)
    own = parts[0] + parts[1] + parts[2] + parts[3]
    state = jnp.concatenate([own[:, TILE:], -dot(own, gain)], axis=1)
    descent = []
    rounds = len(SWAP)
    for j in range(rounds):
        right = ((place >> j) & 1) == 1
        last = j == rounds - 1
        other = swap(maps[TILE:] if last else maps, j, count)
        other_state = swap(state, j, count)
        other_k = other if last else other[TILE:]
        push = jnp.where(
            right,
            other_state[:, :TILE],
            other_state[:, TILE:] + dot(state[:, :TILE], other_k),
        )
        if last:
            descent.append((right, None, push))
            break
        first = jnp.where(right, other, maps)
        second = jnp.where(right, maps, other)
        product = dot(second, first[:TILE])
        turned = dot(first[:TILE], product[TILE:], ((0,), (0,)))
        step = jnp.where(
            right,
            jnp.concatenate([other[:TILE].T, jnp.zeros_like(turned)], axis=0),
            jnp.concatenate([product[TILE:].T, other[:TILE]], axis=0),
        )
        descent.append((right, step, push))
        early = jnp.where(right, other_state, state)
        late = jnp.where(right, state, other_state)
        state = jnp.concatenate(
            [
                late[:, :TILE] + dot(early[:, :TILE], second[:TILE], ((1,), (1,))),
                early[:, TILE:]
                + dot(late[:, TILE:], first[:TILE])
                + dot(early[:, :TILE], product[TILE:]),
            ],
            axis=1,
        )
        maps = jnp.concatenate([product[:TILE], first[TILE:] + turned], axis=0)
    before = jnp.zeros((columns, TILE), jnp.float32)
    after = before
    for right, step, push in reversed(descent):
        if step is not None:
            push = push + dot(jnp.concatenate([before, after], axis=1), step)
        before, after = jnp.where(right, push, before), jnp.where(right, after, push)
    forward = own + dot(before, gain, ((1,), (1,)))
    forward = jnp.concatenate([forward[:, :TILE], forward[:, TILE:] - after], axis=1)
    share = dot(forward, inverse)
    spread = lax.all_to_all(
        jnp.broadcast_to(share[None], (reps,) + share.shape), "rep", 0, 0
    )
    solution = spread.reshape(-1, share.shape[1]).T
    final = subtree_backward(solution, forward_sub, subtree_inverse, live, block, rows)
    return (solution[None], final[None, None])


def solution(mesh):
    return jax.shard_map(
        shards,
        mesh=mesh,
        in_specs=(
            P("chain", "rep", None, None),
            P("chain", "rep", None, None),
            P("chain", "rep"),
            P("chain", "rep", None, None),
            P("chain", "rep", None),
            P("chain", None, None),
            P("chain", None, None),
            P("chain", None, None),
        ),
        out_specs=(P("chain", None, None), P("chain", "rep", None, None)),
        check_vma=False,
    )
```

```python
import functools

import jax
import jax.numpy as jnp
from jax import lax
from jax.experimental import pallas as pl
from jax.experimental.pallas import tpu as pltpu
from jax.sharding import PartitionSpec as P

TILE = 128
HIGHEST = lax.Precision.HIGHEST
SWAP = (1, 2, 6, 8, 16, 32, 96)


def dot(a, b, dims=((1,), (0,)), precision=HIGHEST):
    return lax.dot_general(
        a, b, (dims, ((), ())), precision=precision, preferred_element_type=jnp.float32
    )


def swap(value, j, count):
    return lax.ppermute(value, "chain", [(k, k ^ SWAP[j]) for k in range(count)])


def level_maps(inverse, couple):
    gain = -dot(inverse, couple)
    return gain, jnp.concatenate([gain[TILE:], -dot(gain, gain, ((0,), (0,)))], axis=0)


def live_columns(tiles_ref, rows, columns):
    return lax.broadcasted_iota(jnp.int32, (rows, columns), 1) < TILE * tiles_ref[...]


def subtree_forward_kernel(
    subtree_inverse_ref, rhs_ref, tiles_ref, update_ref, rows_ref, level_rhs_ref, inverse_ref,
    forward_ref, part_ref,
):
    columns, sub_rows = forward_ref.shape
    live = live_columns(tiles_ref, columns, sub_rows)
    masked = jnp.where(live, rhs_ref[...].astype(jnp.float32).T, 0.0).astype(jnp.bfloat16)
    solved = dot(masked, subtree_inverse_ref[...], ((1,), (1,)), None)
    forward = jnp.where(live, solved, 0.0).astype(jnp.bfloat16)
    forward_ref[...] = forward
    contrib = dot(forward, update_ref[...], ((1,), (1,)), None)
    totals = []
    for s in range(inverse_ref.shape[0] // TILE):
        total = jnp.zeros((columns, TILE), jnp.float32)
        for t in range(rows_ref.shape[1]):
            here = rows_ref[:, t : t + 1] == s
            total = total + jnp.where(here, contrib[:, t * TILE : (t + 1) * TILE], 0.0)
        totals.append(total)
    rest = 0.25 * level_rhs_ref[...].T - jnp.concatenate(totals, axis=1)
    part_ref[...] = dot(rest, inverse_ref[...], ((1,), (1,)))


def subtree_backward_kernel(
    solution_ref, forward_ref, subtree_inverse_ref, tiles_ref, update_ref, rows_ref,
    level_ref, final_ref,
):
    columns, sub_rows = forward_ref.shape
    live = live_columns(tiles_ref, columns, sub_rows)
    level_ref[...] = solution_ref[...].T
    picked = []
    for t in range(rows_ref.shape[1]):
        tile = solution_ref[:, :TILE]
        for s in range(1, solution_ref.shape[1] // TILE):
            here = rows_ref[:, t : t + 1] == s
            tile = jnp.where(here, solution_ref[:, s * TILE : (s + 1) * TILE], tile)
        picked.append(tile.astype(jnp.bfloat16))
    pulled = dot(jnp.concatenate(picked, axis=1), update_ref[...], precision=None)
    residue = forward_ref[...].astype(jnp.float32) - jnp.where(live, pulled, 0.0)
    final = dot(residue.astype(jnp.bfloat16), subtree_inverse_ref[...], precision=None)
    final_ref[...] = jnp.where(live, final, 0.0).T


def local_call(kernel, out_shape, *operands):
    vmem = pl.BlockSpec(memory_space=pltpu.VMEM)
    return pl.pallas_call(
        kernel,
        out_shape=out_shape,
        in_specs=[vmem] * len(operands),
        out_specs=[vmem] * len(out_shape),
        compiler_params=pltpu.CompilerParams(vmem_limit_bytes=24 * 2**20),
    )(*operands)


def shards(
    sub_inverse, sub_rhs, sub_tiles, update, update_rows, level_inverse, coupling, level_rhs
):
    count, reps = lax.axis_size("chain"), lax.axis_size("rep")
    place = lax.axis_index("chain")
    subtree_inverse, rhs_sub, block, rows = sub_inverse[0, 0], sub_rhs[0, 0], update[0, 0], update_rows[0]
    inverse, couple, rhs_level = level_inverse[0], coupling[0], level_rhs[0]
    sub_rows, width = subtree_inverse.shape[0], rhs_level.shape[1]
    gain, maps = level_maps(inverse, couple)
    forward_sub, part = local_call(
        subtree_forward_kernel,
        [
            jax.ShapeDtypeStruct((width, sub_rows), jnp.bfloat16),
            jax.ShapeDtypeStruct((width, inverse.shape[0]), jnp.float32),
        ],
        subtree_inverse, rhs_sub, sub_tiles, block, rows, rhs_level, inverse,
    )
    columns = part.shape[0] // reps
    parts = lax.all_to_all(part.reshape(reps, columns, -1), "rep", 0, 0)
    own = parts[0] + parts[1] + parts[2] + parts[3]
    state = jnp.concatenate([own[:, TILE:], -dot(own, gain)], axis=1)
    descent = []
    rounds = len(SWAP)
    for j in range(rounds):
        right = ((place >> j) & 1) == 1
        last = j == rounds - 1
        other = swap(maps[TILE:] if last else maps, j, count)
        other_state = swap(state, j, count)
        other_k = other if last else other[TILE:]
        push = jnp.where(
            right,
            other_state[:, :TILE],
            other_state[:, TILE:] + dot(state[:, :TILE], other_k),
        )
        if last:
            descent.append((right, None, push))
            break
        first = jnp.where(right, other, maps)
        second = jnp.where(right, maps, other)
        product = dot(second, first[:TILE])
        turned = dot(first[:TILE], product[TILE:], ((0,), (0,)))
        step = jnp.where(
            right,
            jnp.concatenate([other[:TILE].T, jnp.zeros_like(turned)], axis=0),
            jnp.concatenate([product[TILE:].T, other[:TILE]], axis=0),
        )
        descent.append((right, step, push))
        early = jnp.where(right, other_state, state)
        late = jnp.where(right, state, other_state)
        state = jnp.concatenate(
            [
                late[:, :TILE] + dot(early[:, :TILE], second[:TILE], ((1,), (1,))),
                early[:, TILE:]
                + dot(late[:, TILE:], first[:TILE])
                + dot(early[:, :TILE], product[TILE:]),
            ],
            axis=1,
        )
        maps = jnp.concatenate([product[:TILE], first[TILE:] + turned], axis=0)
    before = jnp.zeros((columns, TILE), jnp.float32)
    after = before
    for right, step, push in reversed(descent):
        if step is not None:
            push = push + dot(jnp.concatenate([before, after], axis=1), step)
        before, after = jnp.where(right, push, before), jnp.where(right, after, push)
    forward = own + dot(before, gain, ((1,), (1,)))
    forward = jnp.concatenate([forward[:, :TILE], forward[:, TILE:] - after], axis=1)
    share = dot(forward, inverse)
    spread = lax.all_to_all(
        jnp.broadcast_to(share[None], (reps,) + share.shape), "rep", 0, 0
    )
    solution, final = local_call(
        subtree_backward_kernel,
        [
            jax.ShapeDtypeStruct((inverse.shape[0], width), jnp.float32),
            jax.ShapeDtypeStruct((sub_rows, width), jnp.float32),
        ],
        spread.reshape(width, -1), forward_sub, subtree_inverse, sub_tiles, block, rows,
    )
    return (solution[None], final[None, None])


def solution(mesh):
    return jax.shard_map(
        shards,
        mesh=mesh,
        in_specs=(
            P("chain", "rep", None, None),
            P("chain", "rep", None, None),
            P("chain", "rep"),
            P("chain", "rep", None, None),
            P("chain", "rep", None),
            P("chain", None, None),
            P("chain", None, None),
            P("chain", None, None),
        ),
        out_specs=(P("chain", None, None), P("chain", "rep", None, None)),
        check_vma=False,
    )
```

```python
import jax
import jax.numpy as jnp
from jax import lax
from jax.experimental import pallas as pl
from jax.experimental.pallas import tpu as pltpu
from jax.sharding import Mesh, PartitionSpec as P

TILE = 128
HIGHEST = lax.Precision.HIGHEST
SWAP = (1, 3, 4, 8, 16, 48)


def dot(a, b, dims=((1,), (0,)), precision=HIGHEST):
    return lax.dot_general(
        a, b, (dims, ((), ())), precision=precision, preferred_element_type=jnp.float32
    )


def swap(value, j, count):
    return lax.ppermute(value, "pair", [(n, n ^ SWAP[j]) for n in range(count)])


def join_maps(first, second):
    product = dot(second, first[:TILE])
    turned = dot(first[:TILE], product[TILE:], ((0,), (0,)))
    joined = jnp.concatenate([product[:TILE], first[TILE:] + turned], axis=0)
    upper = jnp.concatenate([second[:TILE].T, product[TILE:]], axis=1)
    lower = jnp.concatenate([jnp.zeros_like(turned), first[:TILE]], axis=1)
    return joined, product[TILE:], jnp.concatenate([upper, lower], axis=0)


def join_state(first, second, weights):
    mixed = jnp.concatenate([first[:, :TILE], second[:, TILE:]], axis=1)
    kept = jnp.concatenate([second[:, :TILE], first[:, TILE:]], axis=1)
    return kept + dot(mixed, weights)


def level_state(own, gain):
    return jnp.concatenate([own[:, TILE:], -dot(own, gain)], axis=1)


def level_solve(own, before, after, gain, inverse):
    forward = own + dot(before, gain, ((1,), (1,)))
    forward = jnp.concatenate([forward[:, :TILE], forward[:, TILE:] - after], axis=1)
    return dot(forward, inverse)


def live_columns(tiles_ref, rows, columns):
    return lax.broadcasted_iota(jnp.int32, (rows, columns), 1) < TILE * tiles_ref[...]


def subtree_forward_kernel(
    subtree_inverse_ref, rhs_ref, tiles_ref, update_ref, rows_ref, level_rhs_ref, inverse_ref,
    forward_ref, part_ref,
):
    columns, sub_rows = forward_ref.shape
    live = live_columns(tiles_ref, columns, sub_rows)
    masked = jnp.where(live, rhs_ref[...].astype(jnp.float32).T, 0.0).astype(jnp.bfloat16)
    solved = dot(masked, subtree_inverse_ref[...], ((1,), (1,)), None)
    forward = jnp.where(live, solved, 0.0).astype(jnp.bfloat16)
    forward_ref[...] = forward
    contrib = dot(forward, update_ref[...], ((1,), (1,)), None)
    totals = []
    for s in range(inverse_ref.shape[0] // TILE):
        total = jnp.zeros((columns, TILE), jnp.float32)
        for t in range(rows_ref.shape[1]):
            here = rows_ref[:, t : t + 1] == s
            total = total + jnp.where(here, contrib[:, t * TILE : (t + 1) * TILE], 0.0)
        totals.append(total)
    rest = 0.25 * level_rhs_ref[...].T - jnp.concatenate(totals, axis=1)
    part_ref[...] = dot(rest, inverse_ref[...], ((1,), (1,)))


def subtree_backward_kernel(
    solution_ref, forward_ref, subtree_inverse_ref, tiles_ref, update_ref, rows_ref,
    level_ref, final_ref,
):
    columns, sub_rows = forward_ref.shape
    live = live_columns(tiles_ref, columns, sub_rows)
    level_ref[...] = solution_ref[...].T
    picked = []
    for t in range(rows_ref.shape[1]):
        tile = solution_ref[:, :TILE]
        for s in range(1, solution_ref.shape[1] // TILE):
            here = rows_ref[:, t : t + 1] == s
            tile = jnp.where(here, solution_ref[:, s * TILE : (s + 1) * TILE], tile)
        picked.append(tile.astype(jnp.bfloat16))
    pulled = dot(jnp.concatenate(picked, axis=1), update_ref[...], precision=None)
    residue = forward_ref[...].astype(jnp.float32) - jnp.where(live, pulled, 0.0)
    final = dot(residue.astype(jnp.bfloat16), subtree_inverse_ref[...], precision=None)
    final_ref[...] = jnp.where(live, final, 0.0).T


def local_call(kernel, out_shape, *operands):
    vmem = pl.BlockSpec(memory_space=pltpu.VMEM)
    return pl.pallas_call(
        kernel,
        out_shape=out_shape,
        in_specs=[vmem] * len(operands),
        out_specs=[vmem] * len(out_shape),
        compiler_params=pltpu.CompilerParams(vmem_limit_bytes=10 * 2**20),
    )(*operands)


def shards(
    sub_inverse, sub_rhs, sub_tiles, update, update_rows, level_inverse, coupling, level_rhs
):
    count, place = lax.axis_size("pair"), lax.axis_index("pair")
    odd = lax.axis_index("core") == 1
    group = ("core", "rep")
    members = lax.axis_size(group)
    subtree_inverse, rhs_sub, block, rows = sub_inverse[0, 0], sub_rhs[0, 0], update[0, 0], update_rows[0]
    inverse, couple, rhs_level = level_inverse[0], coupling[0], level_rhs[0]
    sub_rows, width, height = subtree_inverse.shape[0], rhs_level.shape[1], inverse.shape[0]
    gain = -dot(inverse, couple)
    level = jnp.concatenate(
        [
            gain,
            -dot(gain, gain, ((0,), (0,))),
            inverse[:, :TILE],
            inverse[:, TILE:],
        ],
        axis=0,
    )
    sibling = lax.ppermute(level, "core", [(0, 1), (1, 0)])
    levels = (jnp.where(odd, sibling, level), jnp.where(odd, level, sibling))
    gains = [pair[:height] for pair in levels]
    inverses = [
        jnp.concatenate([pair[height + TILE : 2 * height + TILE], pair[2 * height + TILE :]], axis=1)
        for pair in levels
    ]
    pair_maps = [pair[height - TILE : height + TILE] for pair in levels]
    forward_sub, part = local_call(
        subtree_forward_kernel,
        [
            jax.ShapeDtypeStruct((width, sub_rows), jnp.bfloat16),
            jax.ShapeDtypeStruct((width, height), jnp.float32),
        ],
        subtree_inverse, rhs_sub, sub_tiles, block, rows, rhs_level, inverse,
    )
    columns = width // members
    parts = lax.all_to_all(part.reshape(members, columns, height), group, 0, 0)
    reps = members // 2
    owns = [sum(parts[c * reps + r] for r in range(reps)) for c in range(2)]
    states = [level_state(own, g) for own, g in zip(owns, gains)]
    maps, pair_turn, weights = join_maps(*pair_maps)
    state = join_state(*states, weights)
    descent = []
    rounds = len(SWAP)
    for j in range(rounds):
        right = ((place >> j) & 1) == 1
        last = j == rounds - 1
        other = swap(maps[TILE:] if last else maps, j, count)
        other_state = swap(state, j, count)
        other_k = other if last else other[TILE:]
        push = jnp.where(
            right,
            other_state[:, :TILE],
            other_state[:, TILE:] + dot(state[:, :TILE], other_k),
        )
        if last:
            descent.append((right, None, push))
            break
        first = jnp.where(right, other, maps)
        second = jnp.where(right, maps, other)
        maps, turn, weights = join_maps(first, second)
        step = jnp.where(
            right,
            jnp.concatenate([other[:TILE].T, jnp.zeros_like(turn)], axis=0),
            jnp.concatenate([turn.T, other[:TILE]], axis=0),
        )
        descent.append((right, step, push))
        early = jnp.where(right, other_state, state)
        late = jnp.where(right, state, other_state)
        state = join_state(early, late, weights)
    before = jnp.zeros((columns, TILE), jnp.float32)
    after = before
    for right, step, push in reversed(descent):
        if step is not None:
            push = push + dot(jnp.concatenate([before, after], axis=1), step)
        before, after = jnp.where(right, push, before), jnp.where(right, after, push)
    middle_before = states[0][:, :TILE] + dot(before, pair_maps[0][:TILE], ((1,), (1,)))
    middle_after = (
        states[1][:, TILE:]
        + dot(states[0][:, :TILE], pair_maps[1][TILE:])
        + dot(before, pair_turn, ((1,), (1,)))
        + dot(after, pair_maps[1][:TILE])
    )
    shares = [
        level_solve(owns[0], before, middle_after, gains[0], inverses[0]),
        level_solve(owns[1], middle_before, after, gains[1], inverses[1]),
    ]
    spread = lax.all_to_all(
        jnp.stack([shares[c] for c in range(2) for _ in range(reps)]), group, 0, 0
    )
    solution, final = local_call(
        subtree_backward_kernel,
        [
            jax.ShapeDtypeStruct((height, width), jnp.float32),
            jax.ShapeDtypeStruct((sub_rows, width), jnp.float32),
        ],
        spread.reshape(width, -1), forward_sub, subtree_inverse, sub_tiles, block, rows,
    )
    return (solution[None], final[None, None])


def solution(mesh):
    chain, reps = mesh.devices.shape
    split = Mesh(mesh.devices.reshape(chain // 2, 2, reps), ("pair", "core", "rep"))
    both = ("pair", "core")
    return jax.shard_map(
        shards,
        mesh=split,
        in_specs=(
            P(both, "rep", None, None),
            P(both, "rep", None, None),
            P(both, "rep"),
            P(both, "rep", None, None),
            P(both, "rep", None),
            P(both, None, None),
            P(both, None, None),
            P(both, None, None),
        ),
        out_specs=(P(both, None, None), P(both, "rep", None, None)),
        check_vma=False,
    )
```

```python
import functools

import jax
import jax.numpy as jnp
from jax import lax
from jax.experimental import pallas as pl
from jax.experimental.pallas import tpu as pltpu
from jax.sharding import Mesh, PartitionSpec as P

TILE = 128
HIGHEST = lax.Precision.HIGHEST
SWAP = (1, 3, 4, 8, 16, 48)


def dot(a, b, dims=((1,), (0,)), precision=HIGHEST):
    return lax.dot_general(
        a, b, (dims, ((), ())), precision=precision, preferred_element_type=jnp.float32
    )


def swap(value, j, count):
    return lax.ppermute(value, "pair", [(n, n ^ SWAP[j]) for n in range(count)])


def pick(bits_ref, at):
    return bits_ref[at : at + 1, :1] == 1


def level_kernel(inverse_ref, couple_ref, level_ref):
    height = inverse_ref.shape[0]
    gain = -dot(inverse_ref[...], couple_ref[...])
    level_ref[:height] = gain
    level_ref[height : height + TILE] = -dot(gain.T, gain)
    level_ref[height + TILE : 2 * height + TILE] = inverse_ref[:, :TILE]
    level_ref[2 * height + TILE :] = inverse_ref[:, TILE:]


def join_maps(right, first, second, maps_ref, weights_ref, step_ref):
    early = first[:TILE]
    product = dot(second, early)
    turn = product[TILE:]
    maps_ref[:TILE] = product[:TILE]
    flipped = early.T
    maps_ref[TILE:] = first[TILE:] + dot(flipped, turn)
    weights_ref[:TILE, :TILE] = second[:TILE].T
    weights_ref[:TILE, TILE:] = turn
    weights_ref[TILE:, :TILE] = jnp.zeros_like(turn)
    weights_ref[TILE:, TILE:] = early
    if step_ref is not None:
        step_ref[:TILE] = jnp.where(right, flipped, turn.T)
        step_ref[TILE:] = jnp.where(right, 0.0, second[:TILE])


def pair_kernel(bits_ref, level_ref, sibling_ref, maps_ref, weights_ref):
    odd = pick(bits_ref, 0)
    own, other = level_ref[TILE : 3 * TILE], sibling_ref[TILE : 3 * TILE]
    join_maps(
        None, jnp.where(odd, other, own), jnp.where(odd, own, other), maps_ref, weights_ref, None
    )


def maps_kernel(j, bits_ref, own_ref, other_ref, maps_ref, weights_ref, step_ref):
    right = pick(bits_ref, j)
    own, other = own_ref[...], other_ref[...]
    join_maps(
        right, jnp.where(right, other, own), jnp.where(right, own, other),
        maps_ref, weights_ref, step_ref,
    )


def join_state(first, second, weights):
    mixed = jnp.concatenate([first[:, :TILE], second[:, TILE:]], axis=1)
    kept = jnp.concatenate([second[:, :TILE], first[:, TILE:]], axis=1)
    return kept + dot(mixed, weights)


def start_kernel(
    bits_ref, parts_ref, level_ref, sibling_ref, weights_ref, later_ref,
    owns_ref, states_ref, state_ref,
):
    odd = pick(bits_ref, 0)
    reps, height = parts_ref.shape[0] // 2, parts_ref.shape[2]
    own_gain, other_gain = level_ref[:height], sibling_ref[:height]
    gains = (jnp.where(odd, other_gain, own_gain), jnp.where(odd, own_gain, other_gain))
    states = []
    for c in range(2):
        own = parts_ref[c * reps]
        for r in range(1, reps):
            own = own + parts_ref[c * reps + r]
        owns_ref[c] = own
        states.append(jnp.concatenate([own[:, TILE:], -dot(own, gains[c])], axis=1))
        states_ref[c] = states[c]
    state_ref[...] = join_state(states[0], states[1], weights_ref[...])


def state_kernel(j, bits_ref, own_ref, other_ref, weights_ref, *refs):
    right = pick(bits_ref, j)
    own, other = own_ref[...], other_ref[...]
    refs[-1][...] = join_state(
        jnp.where(right, other, own), jnp.where(right, own, other), weights_ref[...]
    )


def descend_kernel(rounds, bits_ref, level_ref, sibling_ref, weights_ref, owns_ref, states_ref, *refs):
    sent, got = refs[:rounds], refs[rounds : 2 * rounds]
    answers, steps = refs[2 * rounds : 3 * rounds], refs[3 * rounds : -1]
    shares_ref = refs[-1]
    odd = pick(bits_ref, 0)
    height = owns_ref.shape[2]
    pushes = []
    for j in range(rounds):
        answer = answers[j][answers[j].shape[0] - TILE :]
        other = got[j][...]
        pushes.append(
            jnp.where(
                pick(bits_ref, j + 1),
                other[:, :TILE],
                other[:, TILE:] + dot(sent[j][:, :TILE], answer),
            )
        )
    before = jnp.zeros_like(pushes[0])
    after = before
    for j in reversed(range(rounds)):
        right, push = pick(bits_ref, j + 1), pushes[j]
        if j < rounds - 1:
            push = push + dot(jnp.concatenate([before, after], axis=1), steps[j][...])
        before, after = jnp.where(right, push, before), jnp.where(right, after, push)
    own, other = level_ref[...], sibling_ref[...]
    levels = (jnp.where(odd, other, own), jnp.where(odd, own, other))
    maps = [level[TILE : 3 * TILE] for level in levels]
    entry = states_ref[0, :, :TILE]
    middle_before = entry + dot(before, maps[0][:TILE], ((1,), (1,)))
    middle_after = (
        states_ref[1, :, TILE:]
        + dot(entry, maps[1][TILE:])
        + dot(before, weights_ref[:TILE, TILE:], ((1,), (1,)))
        + dot(after, maps[1][:TILE])
    )
    reps = shares_ref.shape[0] // 2
    ends = ((before, middle_after), (middle_before, after))
    for c in range(2):
        level = levels[c]
        forward = owns_ref[c] + dot(ends[c][0], level[:height], ((1,), (1,)))
        forward = jnp.concatenate(
            [forward[:, :TILE], forward[:, TILE:] - ends[c][1]], axis=1
        )
        left = dot(forward, level[height + TILE : 2 * height + TILE])
        share = jnp.concatenate([left, dot(forward, level[2 * height + TILE :])], axis=1)
        for r in range(reps):
            shares_ref[c * reps + r] = share


def live_columns(tiles_ref, rows, columns):
    return lax.broadcasted_iota(jnp.int32, (rows, columns), 1) < TILE * tiles_ref[...]


def subtree_forward_kernel(
    subtree_inverse_ref, rhs_ref, tiles_ref, update_ref, rows_ref, level_rhs_ref,
    forward_ref, rest_ref,
):
    columns, sub_rows = forward_ref.shape
    live = live_columns(tiles_ref, columns, sub_rows)
    masked = jnp.where(live, rhs_ref[...].astype(jnp.float32).T, 0.0).astype(jnp.bfloat16)
    solved = dot(masked, subtree_inverse_ref[...], ((1,), (1,)), None)
    forward = jnp.where(live, solved, 0.0).astype(jnp.bfloat16)
    forward_ref[...] = forward
    contrib = dot(forward, update_ref[...], ((1,), (1,)), None)
    totals = []
    for s in range(level_rhs_ref.shape[0] // TILE):
        total = jnp.zeros((columns, TILE), jnp.float32)
        for t in range(rows_ref.shape[1]):
            here = rows_ref[:, t : t + 1] == s
            total = total + jnp.where(here, contrib[:, t * TILE : (t + 1) * TILE], 0.0)
        totals.append(total)
    rest_ref[...] = 0.25 * level_rhs_ref[...].T - jnp.concatenate(totals, axis=1)


def part_kernel(rest_ref, inverse_ref, later_ref, part_ref):
    part_ref[...] = dot(rest_ref[...], inverse_ref[...], ((1,), (1,)))


def subtree_backward_kernel(
    solution_ref, forward_ref, subtree_inverse_ref, tiles_ref, update_ref, rows_ref,
    level_ref, final_ref,
):
    columns, sub_rows = forward_ref.shape
    live = live_columns(tiles_ref, columns, sub_rows)
    level_ref[...] = solution_ref[...].T
    picked = []
    for t in range(rows_ref.shape[1]):
        tile = solution_ref[:, :TILE]
        for s in range(1, solution_ref.shape[1] // TILE):
            here = rows_ref[:, t : t + 1] == s
            tile = jnp.where(here, solution_ref[:, s * TILE : (s + 1) * TILE], tile)
        picked.append(tile.astype(jnp.bfloat16))
    pulled = dot(jnp.concatenate(picked, axis=1), update_ref[...], precision=None)
    residue = forward_ref[...].astype(jnp.float32) - jnp.where(live, pulled, 0.0)
    final = dot(residue.astype(jnp.bfloat16), subtree_inverse_ref[...], precision=None)
    final_ref[...] = jnp.where(live, final, 0.0).T


def local_call(kernel, out_shape, *operands, later=()):
    vmem = pl.BlockSpec(memory_space=pltpu.VMEM)
    return pl.pallas_call(
        kernel,
        out_shape=out_shape,
        in_specs=[vmem] * len(operands) + [pl.BlockSpec(memory_space=pl.ANY)] * len(later),
        out_specs=[vmem] * len(out_shape),
        compiler_params=pltpu.CompilerParams(vmem_limit_bytes=8 * 2**20),
    )(*operands, *later)


def f32(*shape):
    return jax.ShapeDtypeStruct(shape, jnp.float32)


def shards(
    sub_inverse, sub_rhs, sub_tiles, update, update_rows, level_inverse, coupling, level_rhs
):
    count, place = lax.axis_size("pair"), lax.axis_index("pair")
    group = ("core", "rep")
    members = lax.axis_size(group)
    subtree_inverse, rhs_sub, block, rows = sub_inverse[0, 0], sub_rhs[0, 0], update[0, 0], update_rows[0]
    inverse, couple, rhs_level = level_inverse[0], coupling[0], level_rhs[0]
    sub_rows, width, height = subtree_inverse.shape[0], rhs_level.shape[1], inverse.shape[0]
    rounds = len(SWAP)
    spot = 2 * place + lax.axis_index("core")
    bits = (spot >> lax.broadcasted_iota(jnp.int32, (8, 128), 0)) & 1
    (level,) = local_call(level_kernel, [f32(2 * height + height + TILE, TILE)], inverse, couple)
    sibling = lax.ppermute(level, "core", [(0, 1), (1, 0)])
    forward_sub, rest = local_call(
        subtree_forward_kernel,
        [jax.ShapeDtypeStruct((width, sub_rows), jnp.bfloat16), f32(width, height)],
        subtree_inverse, rhs_sub, sub_tiles, block, rows, rhs_level,
    )
    maps, pair_weights = local_call(
        pair_kernel, [f32(2 * TILE, TILE), f32(2 * TILE, 2 * TILE)], bits, level, sibling
    )
    (part,) = local_call(part_kernel, [f32(width, height)], rest, inverse, later=(maps,))
    columns = width // members
    parts = lax.all_to_all(part.reshape(members, columns, height), group, 0, 0)
    answers, weights, steps, chain = [], [], [], [maps]
    for j in range(rounds):
        if j == rounds - 1:
            answers.append(swap(maps[TILE:], j, count))
            break
        answers.append(swap(maps, j, count))
        maps, weight, step = local_call(
            functools.partial(maps_kernel, j + 1),
            [f32(2 * TILE, TILE), f32(2 * TILE, 2 * TILE), f32(2 * TILE, TILE)],
            bits, maps, answers[j],
        )
        weights.append(weight)
        steps.append(step)
        chain.append(maps)
    owns, states, state = local_call(
        start_kernel,
        [f32(2, columns, height), f32(2, columns, 2 * TILE), f32(columns, 2 * TILE)],
        bits, parts, level, sibling, pair_weights, later=(chain[1],),
    )
    sent, got = [], []
    for j in range(rounds):
        sent.append(state)
        got.append(swap(state, j, count))
        if j < rounds - 1:
            (state,) = local_call(
                functools.partial(state_kernel, j + 1),
                [f32(columns, 2 * TILE)],
                bits, state, got[j], weights[j], later=(chain[j + 2],) if j < 2 else (),
            )
    (shares,) = local_call(
        functools.partial(descend_kernel, rounds),
        [f32(members, columns, height)],
        bits, level, sibling, pair_weights, owns, states, *sent, *got, *answers, *steps,
    )
    spread = lax.all_to_all(shares, group, 0, 0)
    solution, final = local_call(
        subtree_backward_kernel,
        [f32(height, width), f32(sub_rows, width)],
        spread.reshape(width, -1), forward_sub, subtree_inverse, sub_tiles, block, rows,
    )
    return (solution[None], final[None, None])


def solution(mesh):
    chain, reps = mesh.devices.shape
    split = Mesh(mesh.devices.reshape(chain // 2, 2, reps), ("pair", "core", "rep"))
    both = ("pair", "core")
    return jax.shard_map(
        shards,
        mesh=split,
        in_specs=(
            P(both, "rep", None, None),
            P(both, "rep", None, None),
            P(both, "rep"),
            P(both, "rep", None, None),
            P(both, "rep", None),
            P(both, None, None),
            P(both, None, None),
            P(both, None, None),
        ),
        out_specs=(P(both, None, None), P(both, "rep", None, None)),
        check_vma=False,
    )
```

```python
import functools

import jax
import jax.numpy as jnp
from jax import lax
from jax.experimental import pallas as pl
from jax.experimental.pallas import tpu as pltpu
from jax.sharding import Mesh, PartitionSpec as P

TILE = 128
HIGHEST = lax.Precision.HIGHEST
SWAP = (1, 3, 4, 8, 16, 48)


MAPS_WEIGHT = 40
STATE_WEIGHT = 3


def dot(a, b, dims=((1,), (0,)), precision=HIGHEST):
    return lax.dot_general(
        a, b, (dims, ((), ())), precision=precision, preferred_element_type=jnp.float32
    )


def swap(value, j, count):
    return lax.ppermute(value, "pair", [(n, n ^ SWAP[j]) for n in range(count)])


def pick(bits_ref, at):
    return bits_ref[at : at + 1, :1] == 1


def fetch(sems, *pairs):
    copies = [
        pltpu.make_async_copy(source, target, sems.at[i])
        for i, (source, target) in enumerate(pairs)
    ]
    for copy in copies:
        copy.start()
    return copies


def level_kernel(inverse_hbm, couple_hbm, level_ref, inverse_ref, couple_ref, sems):
    for copy in fetch(sems, (inverse_hbm, inverse_ref), (couple_hbm, couple_ref)):
        copy.wait()
    height = inverse_ref.shape[0]
    gain = -dot(inverse_ref[...], couple_ref[...])
    level_ref[:height] = gain
    level_ref[height : height + TILE] = -dot(gain.T, gain)
    level_ref[height + TILE : 2 * height + TILE] = inverse_ref[:, :TILE]
    level_ref[2 * height + TILE :] = inverse_ref[:, TILE:]


def join_maps(right, first, second, maps_ref, weights_ref, step_ref):
    early = first[:TILE]
    product = dot(second, early)
    turn = product[TILE:]
    maps_ref[:TILE] = product[:TILE]
    flipped = early.T
    maps_ref[TILE:] = first[TILE:] + dot(flipped, turn)
    weights_ref[:TILE, :TILE] = second[:TILE].T
    weights_ref[:TILE, TILE:] = turn
    weights_ref[TILE:, :TILE] = jnp.zeros_like(turn)
    weights_ref[TILE:, TILE:] = early
    if step_ref is not None:
        step_ref[:TILE] = jnp.where(right, flipped, turn.T)
        step_ref[TILE:] = jnp.where(right, 0.0, second[:TILE])


def pair_kernel(bits_ref, level_ref, sibling_ref, later_ref, maps_ref, weights_ref):
    odd = pick(bits_ref, 0)
    own, other = level_ref[TILE : 3 * TILE], sibling_ref[TILE : 3 * TILE]
    join_maps(
        None, jnp.where(odd, other, own), jnp.where(odd, own, other), maps_ref, weights_ref, None
    )


def maps_kernel(j, bits_ref, own_ref, other_ref, later_ref, maps_ref, weights_ref, step_ref):
    right = pick(bits_ref, j)
    own, other = own_ref[...], other_ref[...]
    join_maps(
        right, jnp.where(right, other, own), jnp.where(right, own, other),
        maps_ref, weights_ref, step_ref,
    )


def join_state(first, second, weights):
    mixed = jnp.concatenate([first[:, :TILE], second[:, TILE:]], axis=1)
    kept = jnp.concatenate([second[:, :TILE], first[:, TILE:]], axis=1)
    return kept + dot(mixed, weights)


def start_kernel(
    bits_ref, parts_ref, level_ref, sibling_ref, weights_ref, later_ref,
    owns_ref, states_ref, state_ref,
):
    odd = pick(bits_ref, 0)
    reps, height = parts_ref.shape[0] // 2, parts_ref.shape[2]
    own_gain, other_gain = level_ref[:height], sibling_ref[:height]
    gains = (jnp.where(odd, other_gain, own_gain), jnp.where(odd, own_gain, other_gain))
    states = []
    for c in range(2):
        own = parts_ref[c * reps]
        for r in range(1, reps):
            own = own + parts_ref[c * reps + r]
        owns_ref[c] = own
        states.append(jnp.concatenate([own[:, TILE:], -dot(own, gains[c])], axis=1))
        states_ref[c] = states[c]
    state_ref[...] = join_state(states[0], states[1], weights_ref[...])


def state_kernel(j, bits_ref, own_ref, other_ref, weights_ref, *refs):
    right = pick(bits_ref, j)
    own, other = own_ref[...], other_ref[...]
    refs[-1][...] = join_state(
        jnp.where(right, other, own), jnp.where(right, own, other), weights_ref[...]
    )


def descend_kernel(rounds, bits_ref, level_ref, sibling_ref, weights_ref, owns_ref, states_ref, *refs):
    sent, got = refs[:rounds], refs[rounds : 2 * rounds]
    answers, steps = refs[2 * rounds : 3 * rounds], refs[3 * rounds : -1]
    shares_ref = refs[-1]
    odd = pick(bits_ref, 0)
    height = owns_ref.shape[2]
    pushes = []
    for j in range(rounds):
        answer = answers[j][answers[j].shape[0] - TILE :]
        other = got[j][...]
        pushes.append(
            jnp.where(
                pick(bits_ref, j + 1),
                other[:, :TILE],
                other[:, TILE:] + dot(sent[j][:, :TILE], answer),
            )
        )
    before = jnp.zeros_like(pushes[0])
    after = before
    for j in reversed(range(rounds)):
        right, push = pick(bits_ref, j + 1), pushes[j]
        if j < rounds - 1:
            push = push + dot(jnp.concatenate([before, after], axis=1), steps[j][...])
        before, after = jnp.where(right, push, before), jnp.where(right, after, push)
    own, other = level_ref[...], sibling_ref[...]
    levels = (jnp.where(odd, other, own), jnp.where(odd, own, other))
    maps = [level[TILE : 3 * TILE] for level in levels]
    entry = states_ref[0, :, :TILE]
    middle_before = entry + dot(before, maps[0][:TILE], ((1,), (1,)))
    middle_after = (
        states_ref[1, :, TILE:]
        + dot(entry, maps[1][TILE:])
        + dot(before, weights_ref[:TILE, TILE:], ((1,), (1,)))
        + dot(after, maps[1][:TILE])
    )
    reps = shares_ref.shape[0] // 2
    ends = ((before, middle_after), (middle_before, after))
    for c in range(2):
        level = levels[c]
        forward = owns_ref[c] + dot(ends[c][0], level[:height], ((1,), (1,)))
        forward = jnp.concatenate(
            [forward[:, :TILE], forward[:, TILE:] - ends[c][1]], axis=1
        )
        left = dot(forward, level[height + TILE : 2 * height + TILE])
        share = jnp.concatenate([left, dot(forward, level[2 * height + TILE :])], axis=1)
        for r in range(reps):
            shares_ref[c * reps + r] = share


def live_columns(tiles_ref, rows, columns):
    return lax.broadcasted_iota(jnp.int32, (rows, columns), 1) < TILE * tiles_ref[...]


def subtree_forward_kernel(
    tiles_hbm, rhs_hbm, subtree_inverse_hbm, update_hbm, rows_hbm, level_rhs_hbm, later_ref,
    forward_ref, rest_ref,
    tiles_ref, rhs_ref, subtree_inverse_ref, update_ref, rows_ref, level_rhs_ref, sems,
):
    copies = fetch(
        sems,
        (tiles_hbm, tiles_ref),
        (rhs_hbm, rhs_ref),
        (subtree_inverse_hbm, subtree_inverse_ref),
        (update_hbm, update_ref),
        (rows_hbm, rows_ref),
        (level_rhs_hbm, level_rhs_ref),
    )
    columns, sub_rows = forward_ref.shape
    copies[0].wait()
    live = live_columns(tiles_ref, columns, sub_rows)
    copies[1].wait()
    masked = jnp.where(live, rhs_ref[...].astype(jnp.float32).T, 0.0).astype(jnp.bfloat16)
    copies[2].wait()
    solved = dot(masked, subtree_inverse_ref[...], ((1,), (1,)), None)
    forward = jnp.where(live, solved, 0.0).astype(jnp.bfloat16)
    forward_ref[...] = forward
    copies[3].wait()
    contrib = dot(forward, update_ref[...], ((1,), (1,)), None)
    copies[4].wait()
    totals = []
    for s in range(level_rhs_ref.shape[0] // TILE):
        total = jnp.zeros((columns, TILE), jnp.float32)
        for t in range(rows_ref.shape[1]):
            here = rows_ref[:, t : t + 1] == s
            total = total + jnp.where(here, contrib[:, t * TILE : (t + 1) * TILE], 0.0)
        totals.append(total)
    copies[5].wait()
    rest_ref[...] = 0.25 * level_rhs_ref[...].T - jnp.concatenate(totals, axis=1)


def part_kernel(rest_ref, level_ref, later_ref, part_ref):
    left = level_ref[3 * TILE : 3 * TILE + rest_ref.shape[1]]
    right = level_ref[3 * TILE + rest_ref.shape[1] :]
    part_ref[...] = dot(rest_ref[:, :TILE], left, ((1,), (1,))) + dot(
        rest_ref[:, TILE:], right, ((1,), (1,))
    )


def subtree_backward_kernel(
    solution_ref, forward_ref, tiles_hbm, rows_hbm, update_hbm, subtree_inverse_hbm,
    level_ref, final_ref,
    tiles_ref, rows_ref, update_ref, subtree_inverse_ref, sems,
):
    copies = fetch(
        sems,
        (tiles_hbm, tiles_ref),
        (rows_hbm, rows_ref),
        (update_hbm, update_ref),
        (subtree_inverse_hbm, subtree_inverse_ref),
    )
    columns, sub_rows = forward_ref.shape
    level_ref[...] = solution_ref[...].T
    copies[0].wait()
    live = live_columns(tiles_ref, columns, sub_rows)
    copies[1].wait()
    picked = []
    for t in range(rows_ref.shape[1]):
        tile = solution_ref[:, :TILE]
        for s in range(1, solution_ref.shape[1] // TILE):
            here = rows_ref[:, t : t + 1] == s
            tile = jnp.where(here, solution_ref[:, s * TILE : (s + 1) * TILE], tile)
        picked.append(tile.astype(jnp.bfloat16))
    copies[2].wait()
    pulled = dot(jnp.concatenate(picked, axis=1), update_ref[...], precision=None)
    residue = forward_ref[...].astype(jnp.float32) - jnp.where(live, pulled, 0.0)
    copies[3].wait()
    final = dot(residue.astype(jnp.bfloat16), subtree_inverse_ref[...], precision=None)
    final_ref[...] = jnp.where(live, final, 0.0).T


def local_call(kernel, out_shape, *operands, fetched=(), later=(), weight=0, limit=8 * 2**20):
    vmem = pl.BlockSpec(memory_space=pltpu.VMEM)
    scratch = [pltpu.VMEM(part.shape, part.dtype) for part in fetched]
    if fetched:
        scratch.append(pltpu.SemaphoreType.DMA((len(fetched),)))
    return pl.pallas_call(
        kernel,
        out_shape=out_shape,
        in_specs=[vmem] * len(operands)
        + [pl.BlockSpec(memory_space=pltpu.HBM)] * len(fetched)
        + [pl.BlockSpec(memory_space=pl.ANY)] * len(later),
        out_specs=[vmem] * len(out_shape),
        scratch_shapes=scratch,
        cost_estimate=pl.CostEstimate(
            flops=weight * 10**9, bytes_accessed=weight * 2**20, transcendentals=0
        ),
        compiler_params=pltpu.CompilerParams(vmem_limit_bytes=limit),
    )(*operands, *fetched, *later)


def f32(*shape):
    return jax.ShapeDtypeStruct(shape, jnp.float32)


def shards(
    sub_inverse, sub_rhs, sub_tiles, update, update_rows, level_inverse, coupling, level_rhs
):
    count, place = lax.axis_size("pair"), lax.axis_index("pair")
    group = ("core", "rep")
    members = lax.axis_size(group)
    subtree_inverse, rhs_sub, block, rows = sub_inverse[0, 0], sub_rhs[0, 0], update[0, 0], update_rows[0]
    inverse, couple, rhs_level = level_inverse[0], coupling[0], level_rhs[0]
    sub_rows, width, height = subtree_inverse.shape[0], rhs_level.shape[1], inverse.shape[0]
    rounds = len(SWAP)
    spot = 2 * place + lax.axis_index("core")
    bits = (spot >> lax.broadcasted_iota(jnp.int32, (8, 128), 0)) & 1
    (level,) = local_call(
        level_kernel, [f32(3 * height + TILE, TILE)], fetched=(inverse, couple)
    )
    sibling = lax.ppermute(level, "core", [(0, 1), (1, 0)])
    forward_sub, rest = local_call(
        subtree_forward_kernel,
        [jax.ShapeDtypeStruct((width, sub_rows), jnp.bfloat16), f32(width, height)],
        fetched=(sub_tiles, rhs_sub, subtree_inverse, block, rows, rhs_level), later=(level,),
    )
    maps, pair_weights = local_call(
        pair_kernel, [f32(2 * TILE, TILE), f32(2 * TILE, 2 * TILE)], bits, level, sibling,
        later=(rest,),
    )
    (part,) = local_call(part_kernel, [f32(width, height)], rest, level, later=(maps,))
    columns = width // members
    parts = lax.all_to_all(part.reshape(members, columns, height), group, 0, 0)
    answers, weights, steps = [], [], []

    def advance_maps(j, maps, *later):
        answers.append(swap(maps, j, count))
        maps, weight, step = local_call(
            functools.partial(maps_kernel, j + 1),
            [f32(2 * TILE, TILE), f32(2 * TILE, 2 * TILE), f32(2 * TILE, TILE)],
            bits, maps, answers[j], later=later, weight=MAPS_WEIGHT,
        )
        weights.append(weight)
        steps.append(step)
        return maps

    maps = advance_maps(0, maps, part)
    owns, states, state = local_call(
        start_kernel,
        [f32(2, columns, height), f32(2, columns, 2 * TILE), f32(columns, 2 * TILE)],
        bits, parts, level, sibling, pair_weights, later=(maps,),
    )
    sent, got = [], []
    for j in range(rounds):
        sent.append(state)
        got.append(swap(state, j, count))
        if j < rounds - 2:
            maps = advance_maps(j + 1, maps, state)
        elif j == rounds - 2:
            answers.append(swap(maps[TILE:], j + 1, count))
        if j < rounds - 1:
            (state,) = local_call(
                functools.partial(state_kernel, j + 1),
                [f32(columns, 2 * TILE)],
                bits, state, got[j], weights[j], later=(maps,) if j < 2 else (),
                weight=STATE_WEIGHT,
            )
    (shares,) = local_call(
        functools.partial(descend_kernel, rounds),
        [f32(members, columns, height)],
        bits, level, sibling, pair_weights, owns, states, *sent, *got, *answers, *steps,
    )
    spread = lax.all_to_all(shares, group, 0, 0)
    solution, final = local_call(
        subtree_backward_kernel,
        [f32(height, width), f32(sub_rows, width)],
        spread.reshape(width, -1), forward_sub,
        fetched=(sub_tiles, rows, block, subtree_inverse), limit=66 * 10**6,
    )
    return (solution[None], final[None, None])


def solution(mesh):
    chain, reps = mesh.devices.shape
    split = Mesh(mesh.devices.reshape(chain // 2, 2, reps), ("pair", "core", "rep"))
    both = ("pair", "core")
    return jax.shard_map(
        shards,
        mesh=split,
        in_specs=(
            P(both, "rep", None, None),
            P(both, "rep", None, None),
            P(both, "rep"),
            P(both, "rep", None, None),
            P(both, "rep", None),
            P(both, None, None),
            P(both, None, None),
            P(both, None, None),
        ),
        out_specs=(P(both, None, None), P(both, "rep", None, None)),
        check_vma=False,
    )
```

```python
import functools

import jax
import jax.numpy as jnp
from jax import lax
from jax.experimental import pallas as pl
from jax.experimental.pallas import tpu as pltpu
from jax.sharding import Mesh, PartitionSpec as P

TILE = 128
HALF = TILE // 2
HIGHEST = lax.Precision.HIGHEST
SWAP = (1, 3, 4, 8, 16, 48)


PACKED = 3
MAPS_WEIGHT = 10
STATE_WEIGHT = 1


def dot(a, b, dims=((1,), (0,)), precision=HIGHEST):
    return lax.dot_general(
        a, b, (dims, ((), ())), precision=precision, preferred_element_type=jnp.float32
    )


def swap(value, j, count):
    return lax.ppermute(value, "pair", [(n, n ^ SWAP[j]) for n in range(count)])


def pick(bits_ref, at):
    return bits_ref[at : at + 1, :1] == 1


def fetch(sems, *pairs):
    copies = [
        pltpu.make_async_copy(source, target, sems.at[i])
        for i, (source, target) in enumerate(pairs)
    ]
    for copy in copies:
        copy.start()
    return copies


def corners():
    row = lax.broadcasted_iota(jnp.int32, (HALF, TILE), 0)
    lane = lax.broadcasted_iota(jnp.int32, (HALF, TILE), 1)
    return row, lane


def pack(square):
    row, lane = corners()
    top, bottom = square[:HALF], square[HALF:]
    body = jnp.where((lane >= HALF) & (row > lane - HALF), pltpu.roll(top, HALF, 1), bottom)
    diagonal = jnp.sum(jnp.where(row == lane, top, 0.0), axis=0, keepdims=True)
    return jnp.concatenate([body, jnp.broadcast_to(diagonal, (8, TILE))], axis=0)


def unpack(packed):
    row, lane = corners()
    body, diagonal = packed[:HALF], packed[HALF : HALF + 1]
    first = jnp.where((lane < HALF) & (row > lane), pltpu.roll(body, HALF, 1), 0.0)
    first = jnp.where(row == lane, 0.5 * diagonal, first)
    last = jnp.where((lane < HALF) | (row < lane - HALF), body, 0.0)
    last = jnp.where(row == lane - HALF, 0.5 * body, last)
    half = jnp.concatenate([first, last], axis=0)
    return half + half.T


def join_maps(right, first, second, maps_ref, weights_ref, step_ref=None):
    early = first[:TILE]
    product = dot(second, early)
    turn = product[TILE:]
    flipped = early.T
    answer = first[TILE:] + dot(flipped, turn)
    maps_ref[:TILE] = product[:TILE]
    maps_ref[TILE:] = answer
    weights_ref[:TILE, :TILE] = second[:TILE].T
    weights_ref[:TILE, TILE:] = turn
    weights_ref[TILE:, :TILE] = jnp.zeros_like(turn)
    weights_ref[TILE:, TILE:] = early
    if step_ref is not None:
        step_ref[:TILE] = jnp.where(right, flipped, turn.T)
        step_ref[TILE:] = jnp.where(right, 0.0, second[:TILE])
    return product[:TILE], answer


def pair_kernel(bits_ref, level_ref, sibling_ref, maps_ref, weights_ref):
    odd = pick(bits_ref, 0)
    own, other = level_ref[TILE : 3 * TILE], sibling_ref[TILE : 3 * TILE]
    join_maps(
        odd, jnp.where(odd, other, own), jnp.where(odd, own, other), maps_ref, weights_ref
    )


def maps_kernel(j, later, bits_ref, own_ref, other_ref, *refs):
    maps_ref, weights_ref, step_ref, answer_ref, *message = refs[later:]
    right = pick(bits_ref, j + 1)
    own, other = own_ref[...], other_ref[...]
    if j >= PACKED:
        other = jnp.concatenate([other[:TILE], unpack(other[TILE:])], axis=0)
    answer_ref[...] = other[TILE:]
    ahead, answer = join_maps(
        right, jnp.where(right, other, own), jnp.where(right, own, other),
        maps_ref, weights_ref, step_ref,
    )
    if j + 1 >= PACKED:
        packed = pack(answer)
        if j + 2 < len(SWAP):
            packed = jnp.concatenate([ahead, packed], axis=0)
        message[0][...] = packed


def join_state(first, second, weights):
    mixed = jnp.concatenate([first[:, :TILE], second[:, TILE:]], axis=1)
    kept = jnp.concatenate([second[:, :TILE], first[:, TILE:]], axis=1)
    return kept + dot(mixed, weights)


def start_kernel(
    bits_ref, parts_ref, level_ref, sibling_ref, weights_ref,
    owns_ref, states_ref, state_ref,
):
    odd = pick(bits_ref, 0)
    reps, height = parts_ref.shape[0] // 2, parts_ref.shape[2]
    own_gain, other_gain = level_ref[:height], sibling_ref[:height]
    gains = (jnp.where(odd, other_gain, own_gain), jnp.where(odd, own_gain, other_gain))
    states = []
    for c in range(2):
        own = parts_ref[c * reps]
        for r in range(1, reps):
            own = own + parts_ref[c * reps + r]
        owns_ref[c] = own
        states.append(jnp.concatenate([own[:, TILE:], -dot(own, gains[c])], axis=1))
        states_ref[c] = states[c]
    state_ref[...] = join_state(states[0], states[1], weights_ref[...])


def state_kernel(j, bits_ref, own_ref, other_ref, weights_ref, *refs):
    right = pick(bits_ref, j)
    own, other = own_ref[...], other_ref[...]
    refs[-1][...] = join_state(
        jnp.where(right, other, own), jnp.where(right, own, other), weights_ref[...]
    )


def descend_kernel(rounds, bits_ref, level_ref, sibling_ref, weights_ref, owns_ref, states_ref, *refs):
    sent, got = refs[:rounds], refs[rounds : 2 * rounds]
    answers, steps = refs[2 * rounds : 3 * rounds], refs[3 * rounds : -1]
    shares_ref = refs[-1]
    odd = pick(bits_ref, 0)
    height = owns_ref.shape[2]
    pushes = []
    for j in range(rounds):
        answer = answers[j][...] if j < rounds - 1 else unpack(answers[j][...])
        other = got[j][...]
        pushes.append(
            jnp.where(
                pick(bits_ref, j + 1),
                other[:, :TILE],
                other[:, TILE:] + dot(sent[j][:, :TILE], answer),
            )
        )
    before = jnp.zeros_like(pushes[0])
    after = before
    for j in reversed(range(rounds)):
        right, push = pick(bits_ref, j + 1), pushes[j]
        if j < rounds - 1:
            push = push + dot(jnp.concatenate([before, after], axis=1), steps[j][...])
        before, after = jnp.where(right, push, before), jnp.where(right, after, push)
    own, other = level_ref[...], sibling_ref[...]
    levels = (jnp.where(odd, other, own), jnp.where(odd, own, other))
    maps = [level[TILE : 3 * TILE] for level in levels]
    entry = states_ref[0, :, :TILE]
    middle_before = entry + dot(before, maps[0][:TILE], ((1,), (1,)))
    middle_after = (
        states_ref[1, :, TILE:]
        + dot(entry, maps[1][TILE:])
        + dot(before, weights_ref[:TILE, TILE:], ((1,), (1,)))
        + dot(after, maps[1][:TILE])
    )
    reps = shares_ref.shape[0] // 2
    ends = ((before, middle_after), (middle_before, after))
    for c in range(2):
        level = levels[c]
        forward = owns_ref[c] + dot(ends[c][0], level[:height], ((1,), (1,)))
        forward = jnp.concatenate(
            [forward[:, :TILE], forward[:, TILE:] - ends[c][1]], axis=1
        )
        left = dot(forward, level[height + TILE : 2 * height + TILE])
        share = jnp.concatenate([left, dot(forward, level[2 * height + TILE :])], axis=1)
        for r in range(reps):
            shares_ref[c * reps + r] = share


def live_columns(tiles_ref, rows, columns):
    return lax.broadcasted_iota(jnp.int32, (rows, columns), 1) < TILE * tiles_ref[...]


def first_kernel(
    inverse_hbm, couple_hbm, rhs_hbm, tiles_hbm, subtree_inverse_hbm, update_hbm, rows_hbm,
    level_rhs_hbm,
    level_ref, forward_ref, part_ref,
    inverse_ref, couple_ref, rhs_ref, tiles_ref, subtree_inverse_ref, update_ref, rows_ref,
    level_rhs_ref, sems,
):
    copies = fetch(
        sems,
        (inverse_hbm, inverse_ref),
        (couple_hbm, couple_ref),
        (rhs_hbm, rhs_ref),
        (tiles_hbm, tiles_ref),
        (subtree_inverse_hbm, subtree_inverse_ref),
        (update_hbm, update_ref),
        (rows_hbm, rows_ref),
        (level_rhs_hbm, level_rhs_ref),
    )
    height = inverse_ref.shape[0]
    copies[0].wait()
    copies[1].wait()
    gain = -dot(inverse_ref[...], couple_ref[...])
    level_ref[:height] = gain
    level_ref[height : height + TILE] = -dot(gain.T, gain)
    level_ref[height + TILE : 2 * height + TILE] = inverse_ref[:, :TILE]
    level_ref[2 * height + TILE :] = inverse_ref[:, TILE:]
    columns, sub_rows = forward_ref.shape
    copies[2].wait()
    copies[3].wait()
    live = live_columns(tiles_ref, columns, sub_rows)
    masked = jnp.where(live, rhs_ref[...].astype(jnp.float32).T, 0.0).astype(jnp.bfloat16)
    copies[4].wait()
    solved = dot(masked, subtree_inverse_ref[...], ((1,), (1,)), None)
    forward = jnp.where(live, solved, 0.0).astype(jnp.bfloat16)
    forward_ref[...] = forward
    copies[5].wait()
    contrib = dot(forward, update_ref[...], ((1,), (1,)), None)
    copies[6].wait()
    totals = []
    for s in range(level_rhs_ref.shape[0] // TILE):
        total = jnp.zeros((columns, TILE), jnp.float32)
        for t in range(rows_ref.shape[1]):
            here = rows_ref[:, t : t + 1] == s
            total = total + jnp.where(here, contrib[:, t * TILE : (t + 1) * TILE], 0.0)
        totals.append(total)
    copies[7].wait()
    rest = 0.25 * level_rhs_ref[...].T - jnp.concatenate(totals, axis=1)
    part_ref[...] = dot(rest, inverse_ref[...], ((1,), (1,)))


def subtree_backward_kernel(
    solution_ref, forward_ref, subtree_inverse_ref, tiles_ref, update_ref, rows_ref,
    level_ref, final_ref,
):
    columns, sub_rows = forward_ref.shape
    live = live_columns(tiles_ref, columns, sub_rows)
    level_ref[...] = solution_ref[...].T
    picked = []
    for t in range(rows_ref.shape[1]):
        tile = solution_ref[:, :TILE]
        for s in range(1, solution_ref.shape[1] // TILE):
            here = rows_ref[:, t : t + 1] == s
            tile = jnp.where(here, solution_ref[:, s * TILE : (s + 1) * TILE], tile)
        picked.append(tile.astype(jnp.bfloat16))
    pulled = dot(jnp.concatenate(picked, axis=1), update_ref[...], precision=None)
    residue = forward_ref[...].astype(jnp.float32) - jnp.where(live, pulled, 0.0)
    final = dot(residue.astype(jnp.bfloat16), subtree_inverse_ref[...], precision=None)
    final_ref[...] = jnp.where(live, final, 0.0).T


def local_call(kernel, out_shape, *operands, fetched=(), later=(), weight=0, limit=8 * 2**20):
    vmem = pl.BlockSpec(memory_space=pltpu.VMEM)
    scratch = [pltpu.VMEM(part.shape, part.dtype) for part in fetched]
    if fetched:
        scratch.append(pltpu.SemaphoreType.DMA((len(fetched),)))
    return pl.pallas_call(
        kernel,
        out_shape=out_shape,
        in_specs=[vmem] * len(operands)
        + [pl.BlockSpec(memory_space=pltpu.HBM)] * len(fetched)
        + [pl.BlockSpec(memory_space=pl.ANY)] * len(later),
        out_specs=[vmem] * len(out_shape),
        scratch_shapes=scratch,
        cost_estimate=pl.CostEstimate(
            flops=weight * 10**9, bytes_accessed=weight * 2**20, transcendentals=0
        ),
        compiler_params=pltpu.CompilerParams(vmem_limit_bytes=limit),
    )(*operands, *fetched, *later)


def f32(*shape):
    return jax.ShapeDtypeStruct(shape, jnp.float32)


def shards(
    sub_inverse, sub_rhs, sub_tiles, update, update_rows, level_inverse, coupling, level_rhs
):
    count, place = lax.axis_size("pair"), lax.axis_index("pair")
    group = ("core", "rep")
    members = lax.axis_size(group)
    subtree_inverse, rhs_sub, block, rows = sub_inverse[0, 0], sub_rhs[0, 0], update[0, 0], update_rows[0]
    inverse, couple, rhs_level = level_inverse[0], coupling[0], level_rhs[0]
    sub_rows, width, height = subtree_inverse.shape[0], rhs_level.shape[1], inverse.shape[0]
    rounds = len(SWAP)
    spot = 2 * place + lax.axis_index("core")
    bits = (spot >> lax.broadcasted_iota(jnp.int32, (8, 128), 0)) & 1
    level, forward_sub, part = local_call(
        first_kernel,
        [
            f32(3 * height + TILE, TILE),
            jax.ShapeDtypeStruct((width, sub_rows), jnp.bfloat16),
            f32(width, height),
        ],
        fetched=(inverse, couple, rhs_sub, sub_tiles, subtree_inverse, block, rows, rhs_level),
        limit=66 * 10**6,
    )
    sibling = lax.ppermute(level, "core", [(0, 1), (1, 0)])
    maps, pair_weights = local_call(
        pair_kernel, [f32(2 * TILE, TILE), f32(2 * TILE, 2 * TILE)], bits, level, sibling
    )
    columns = width // members
    parts = lax.all_to_all(part.reshape(members, columns, height), group, 0, 0)
    answers, weights, steps = [], [], []

    def advance_maps(j, maps, message, *later):
        other = swap(message, j, count)
        shapes = [
            f32(2 * TILE, TILE), f32(2 * TILE, 2 * TILE), f32(2 * TILE, TILE), f32(TILE, TILE)
        ]
        if j + 1 >= PACKED:
            shapes.append(f32(HALF + 8 + (TILE if j + 2 < rounds else 0), TILE))
        maps, weight, step, answer, *message = local_call(
            functools.partial(maps_kernel, j, len(later)),
            shapes, bits, maps, other, later=later, weight=MAPS_WEIGHT,
        )
        weights.append(weight)
        steps.append(step)
        answers.append(answer)
        return maps, message[0] if message else maps

    maps, message = advance_maps(0, maps, maps, parts)
    owns, states, state = local_call(
        start_kernel,
        [f32(2, columns, height), f32(2, columns, 2 * TILE), f32(columns, 2 * TILE)],
        bits, parts, level, sibling, pair_weights,
    )
    sent, got = [], []
    for j in range(rounds):
        sent.append(state)
        got.append(swap(state, j, count))
        if j < rounds - 2:
            maps, message = advance_maps(j + 1, maps, message, state)
        elif j == rounds - 2:
            answers.append(swap(message, j + 1, count))
        if j < rounds - 1:
            (state,) = local_call(
                functools.partial(state_kernel, j + 1),
                [f32(columns, 2 * TILE)],
                bits, state, got[j], weights[j], later=(maps,) if j < 1 else (),
                weight=STATE_WEIGHT,
            )
    (shares,) = local_call(
        functools.partial(descend_kernel, rounds),
        [f32(members, columns, height)],
        bits, level, sibling, pair_weights, owns, states, *sent, *got, *answers, *steps,
    )
    spread = lax.all_to_all(shares, group, 0, 0)
    solution, final = local_call(
        subtree_backward_kernel,
        [f32(height, width), f32(sub_rows, width)],
        spread.reshape(width, -1), forward_sub, subtree_inverse, sub_tiles, block, rows,
    )
    return (solution[None], final[None, None])


def solution(mesh):
    chain, reps = mesh.devices.shape
    split = Mesh(mesh.devices.reshape(chain // 2, 2, reps), ("pair", "core", "rep"))
    both = ("pair", "core")
    return jax.shard_map(
        shards,
        mesh=split,
        in_specs=(
            P(both, "rep", None, None),
            P(both, "rep", None, None),
            P(both, "rep"),
            P(both, "rep", None, None),
            P(both, "rep", None),
            P(both, None, None),
            P(both, None, None),
            P(both, None, None),
        ),
        out_specs=(P(both, None, None), P(both, "rep", None, None)),
        check_vma=False,
    )
```

```python
import functools

import jax
import jax.numpy as jnp
from jax import lax
from jax.experimental import pallas as pl
from jax.experimental.pallas import tpu as pltpu
from jax.sharding import Mesh, PartitionSpec as P

TILE = 128
HALF = TILE // 2
MARKS = 16
HIGHEST = lax.Precision.HIGHEST
SWAP = (1, 3, 4, 8, 16, 48)


PACKED = 3
MAPS_WEIGHT = (3, 10, 0, 30, 30)
STATE_WEIGHT = (30, 10, 30, 10, 30)
BEHIND = (True, True, False, True)


def dot(a, b, dims=((1,), (0,)), precision=HIGHEST):
    return lax.dot_general(
        a, b, (dims, ((), ())), precision=precision, preferred_element_type=jnp.float32
    )


def swap(value, j, count):
    return lax.ppermute(value, "pair", [(n, n ^ SWAP[j]) for n in range(count)])


def pick(bits_ref, at):
    return bits_ref[at : at + 1, :1] == 1


def fetch(sems, *pairs):
    copies = [
        pltpu.make_async_copy(source, target, sems.at[i])
        for i, (source, target) in enumerate(pairs)
    ]
    for copy in copies:
        copy.start()
    return copies


def corners():
    row = lax.broadcasted_iota(jnp.int32, (HALF, TILE), 0)
    lane = lax.broadcasted_iota(jnp.int32, (HALF, TILE), 1)
    return row, lane


def pack(square):
    row, lane = corners()
    top, bottom = square[:HALF], square[HALF:]
    body = jnp.where((lane >= HALF) & (row > lane - HALF), pltpu.roll(top, HALF, 1), bottom)
    diagonal = jnp.sum(jnp.where(row == lane, top, 0.0), axis=0, keepdims=True)
    return jnp.concatenate([body, jnp.broadcast_to(diagonal, (8, TILE))], axis=0)


def unpack(packed):
    row, lane = corners()
    body, diagonal = packed[:HALF], packed[HALF : HALF + 1]
    first = jnp.where((lane < HALF) & (row > lane), pltpu.roll(body, HALF, 1), 0.0)
    first = jnp.where(row == lane, 0.5 * diagonal, first)
    last = jnp.where((lane < HALF) | (row < lane - HALF), body, 0.0)
    last = jnp.where(row == lane - HALF, 0.5 * body, last)
    half = jnp.concatenate([first, last], axis=0)
    return half + half.T


def join_maps(right, first, second, maps_ref, weights_ref, step_ref=None):
    early = first[:TILE]
    product = dot(second, early)
    turn = product[TILE:]
    flipped = early.T
    answer = first[TILE:] + dot(flipped, turn)
    if maps_ref is not None:
        maps_ref[:TILE] = product[:TILE]
        maps_ref[TILE:] = answer
    weights_ref[:TILE, :TILE] = second[:TILE].T
    weights_ref[:TILE, TILE:] = turn
    weights_ref[TILE:, :TILE] = jnp.zeros_like(turn)
    weights_ref[TILE:, TILE:] = early
    if step_ref is not None:
        step_ref[:TILE] = jnp.where(right, flipped, turn.T)
        step_ref[TILE:] = jnp.where(right, 0.0, second[:TILE])
    return product[:TILE], answer


def pair_kernel(bits_ref, level_ref, sibling_ref, maps_ref, weights_ref):
    odd = pick(bits_ref, 0)
    own, other = level_ref[TILE : 3 * TILE], sibling_ref[TILE : 3 * TILE]
    join_maps(
        odd, jnp.where(odd, other, own), jnp.where(odd, own, other), maps_ref, weights_ref
    )


def maps_kernel(j, later, bits_ref, own_ref, other_ref, *refs):
    weights_ref, step_ref, answer_ref, *rest = refs[later:]
    right = pick(bits_ref, j + 1)
    own, other = own_ref[...], other_ref[...]
    if j >= PACKED:
        other = jnp.concatenate([other[:TILE], unpack(other[TILE:])], axis=0)
    answer_ref[...] = other[TILE:]
    ahead, answer = join_maps(
        right, jnp.where(right, other, own), jnp.where(right, own, other),
        rest[0] if j + 2 < len(SWAP) else None, weights_ref, step_ref,
    )
    if j + 1 >= PACKED:
        packed = pack(answer)
        if j + 2 < len(SWAP):
            packed = jnp.concatenate([ahead, packed], axis=0)
        rest[-1][...] = packed


def join_state(first, second, weights):
    mixed = jnp.concatenate([first[:, :TILE], second[:, TILE:]], axis=1)
    kept = jnp.concatenate([second[:, :TILE], first[:, TILE:]], axis=1)
    return kept + dot(mixed, weights)


def start_kernel(
    bits_ref, parts_ref, level_ref, sibling_ref, weights_ref,
    owns_ref, states_ref, state_ref,
):
    odd = pick(bits_ref, 0)
    reps, height = parts_ref.shape[0] // 2, parts_ref.shape[2]
    own_gain, other_gain = level_ref[:height], sibling_ref[:height]
    gains = (jnp.where(odd, other_gain, own_gain), jnp.where(odd, own_gain, other_gain))
    states = []
    for c in range(2):
        own = parts_ref[c * reps]
        for r in range(1, reps):
            own = own + parts_ref[c * reps + r]
        owns_ref[c] = own
        states.append(jnp.concatenate([own[:, TILE:], -dot(own, gains[c])], axis=1))
        states_ref[c] = states[c]
    state_ref[...] = join_state(states[0], states[1], weights_ref[...])


def state_kernel(j, bits_ref, own_ref, other_ref, weights_ref, *refs):
    right = pick(bits_ref, j)
    own, other = own_ref[...], other_ref[...]
    refs[-1][...] = join_state(
        jnp.where(right, other, own), jnp.where(right, own, other), weights_ref[...]
    )


def descend_kernel(rounds, bits_ref, level_ref, sibling_ref, weights_ref, owns_ref, states_ref, *refs):
    sent, got = refs[:rounds], refs[rounds : 2 * rounds]
    answers, steps = refs[2 * rounds : 3 * rounds], refs[3 * rounds : 4 * rounds]
    descent_ref = refs[-1]
    odd = pick(bits_ref, 0)
    height = owns_ref.shape[2]
    pushes = []
    for j in range(rounds):
        other = got[j][...]
        pushes.append(
            jnp.where(
                pick(bits_ref, j + 1),
                other[:, :TILE],
                other[:, TILE:] + dot(sent[j][:, :TILE], answers[j][...]),
            )
        )

    def under(constant):
        return jnp.concatenate([jnp.zeros((TILE, constant.shape[1]), jnp.float32), constant], axis=0)

    row = lax.broadcasted_iota(jnp.int32, (TILE + owns_ref.shape[1], TILE), 0)
    lane = lax.broadcasted_iota(jnp.int32, (TILE + owns_ref.shape[1], TILE), 1)
    basis = jnp.where(row == lane, 1.0, 0.0)
    right = pick(bits_ref, rounds + 1)
    before, after = jnp.where(right, basis, 0.0), jnp.where(right, 0.0, basis)
    for j in reversed(range(rounds)):
        right = pick(bits_ref, j + 1)
        push = under(pushes[j]) + dot(jnp.concatenate([before, after], axis=1), steps[j][...])
        before, after = jnp.where(right, push, before), jnp.where(right, after, push)
    own, other = level_ref[...], sibling_ref[...]
    levels = (jnp.where(odd, other, own), jnp.where(odd, own, other))
    maps = [level[TILE : 3 * TILE] for level in levels]
    entry = states_ref[0, :, :TILE]
    middle_before = under(entry) + dot(before, maps[0][:TILE], ((1,), (1,)))
    middle_after = (
        under(states_ref[1, :, TILE:] + dot(entry, maps[1][TILE:]))
        + dot(before, weights_ref[:TILE, TILE:], ((1,), (1,)))
        + dot(after, maps[1][:TILE])
    )
    ends = ((before, middle_after), (middle_before, after))
    for c in range(2):
        level = levels[c]
        forward = under(owns_ref[c]) + dot(ends[c][0], level[:height], ((1,), (1,)))
        forward = jnp.concatenate(
            [forward[:, :TILE], forward[:, TILE:] - ends[c][1]], axis=1
        )
        descent_ref[:, 2 * c * TILE : (2 * c + 1) * TILE] = dot(
            forward, level[height + TILE : 2 * height + TILE]
        )
        descent_ref[:, (2 * c + 1) * TILE : (2 * c + 2) * TILE] = dot(
            forward, level[2 * height + TILE :]
        )


def finish_kernel(rounds, bits_ref, sent_ref, got_ref, answer_ref, descent_ref, shares_ref):
    other = got_ref[...]
    push = jnp.where(
        pick(bits_ref, rounds),
        other[:, :TILE],
        other[:, TILE:] + dot(sent_ref[:, :TILE], unpack(answer_ref[...])),
    )
    both = descent_ref[TILE:] + dot(push, descent_ref[:TILE])
    reps, height = shares_ref.shape[0] // 2, shares_ref.shape[2]
    for c in range(2):
        for r in range(reps):
            shares_ref[c * reps + r] = both[:, c * height : (c + 1) * height]


def live_columns(tiles, rows, columns):
    return lax.broadcasted_iota(jnp.int32, (rows, columns), 1) < TILE * tiles


def first_kernel(
    inverse_hbm, couple_hbm, rhs_hbm, tiles_hbm, subtree_inverse_hbm, update_hbm, rows_hbm,
    level_rhs_hbm,
    level_ref, forward_ref, part_ref,
    inverse_ref, couple_ref, rhs_ref, tiles_ref, subtree_inverse_ref, update_ref, rows_ref,
    level_rhs_ref, sems,
):
    copies = fetch(
        sems,
        (inverse_hbm, inverse_ref),
        (couple_hbm, couple_ref),
        (rhs_hbm, rhs_ref),
        (tiles_hbm, tiles_ref),
        (subtree_inverse_hbm, subtree_inverse_ref),
        (update_hbm, update_ref),
        (rows_hbm, rows_ref),
        (level_rhs_hbm, level_rhs_ref),
    )
    height = inverse_ref.shape[0]
    copies[0].wait()
    copies[1].wait()
    gain = -dot(inverse_ref[...], couple_ref[...])
    level_ref[:height] = gain
    level_ref[height : height + TILE] = -dot(gain.T, gain)
    level_ref[height + TILE : 2 * height + TILE] = inverse_ref[:, :TILE]
    level_ref[2 * height + TILE :] = inverse_ref[:, TILE:]
    columns, sub_rows = rhs_ref.shape[1], rhs_ref.shape[0]
    copies[2].wait()
    copies[3].wait()
    live = live_columns(tiles_ref[...], columns, sub_rows)
    masked = jnp.where(live, rhs_ref[...].astype(jnp.float32).T, 0.0).astype(jnp.bfloat16)
    copies[4].wait()
    solved = dot(masked, subtree_inverse_ref[...], ((1,), (1,)), None)
    forward = jnp.where(live, solved, 0.0).astype(jnp.bfloat16)
    forward_ref[:columns] = forward
    copies[5].wait()
    contrib = dot(forward, update_ref[...], ((1,), (1,)), None)
    copies[6].wait()
    totals = []
    for s in range(level_rhs_ref.shape[0] // TILE):
        total = jnp.zeros((columns, TILE), jnp.float32)
        for t in range(rows_ref.shape[1]):
            here = rows_ref[:, t : t + 1] == s
            total = total + jnp.where(here, contrib[:, t * TILE : (t + 1) * TILE], 0.0)
        totals.append(total)
    row = lax.broadcasted_iota(jnp.int32, (MARKS, sub_rows), 0)
    lane = lax.broadcasted_iota(jnp.int32, (MARKS, sub_rows), 1)
    marks = jnp.where(row == 0, tiles_ref[...], 0)
    for t in range(rows_ref.shape[1]):
        marks = jnp.where((row == 1) & (lane == t), rows_ref[:, t : t + 1], marks)
    forward_ref[columns:] = marks.astype(jnp.float32).astype(jnp.bfloat16)
    copies[7].wait()
    rest = 0.25 * level_rhs_ref[...].T - jnp.concatenate(totals, axis=1)
    part_ref[...] = dot(rest, inverse_ref[...], ((1,), (1,)))


def subtree_backward_kernel(
    solution_ref, forward_ref, subtree_inverse_ref, update_ref, level_ref, final_ref
):
    columns, sub_rows = solution_ref.shape[0], forward_ref.shape[1]
    marks = forward_ref[columns:].astype(jnp.float32).astype(jnp.int32)
    live = live_columns(marks[:1, :1], columns, sub_rows)
    level_ref[...] = solution_ref[...].T
    picked = []
    for t in range(update_ref.shape[0] // TILE):
        tile = solution_ref[:, :TILE]
        for s in range(1, solution_ref.shape[1] // TILE):
            here = marks[1:2, t : t + 1] == s
            tile = jnp.where(here, solution_ref[:, s * TILE : (s + 1) * TILE], tile)
        picked.append(tile.astype(jnp.bfloat16))
    pulled = dot(jnp.concatenate(picked, axis=1), update_ref[...], precision=None)
    residue = forward_ref[:columns].astype(jnp.float32) - jnp.where(live, pulled, 0.0)
    final = dot(residue.astype(jnp.bfloat16), subtree_inverse_ref[...], precision=None)
    final_ref[...] = jnp.where(live, final, 0.0).T


def local_call(kernel, out_shape, *operands, fetched=(), later=(), weight=0, limit=8 * 2**20):
    vmem = pl.BlockSpec(memory_space=pltpu.VMEM)
    scratch = [pltpu.VMEM(part.shape, part.dtype) for part in fetched]
    if fetched:
        scratch.append(pltpu.SemaphoreType.DMA((len(fetched),)))
    return pl.pallas_call(
        kernel,
        out_shape=out_shape,
        in_specs=[vmem] * len(operands)
        + [pl.BlockSpec(memory_space=pltpu.HBM)] * len(fetched)
        + [pl.BlockSpec(memory_space=pl.ANY)] * len(later),
        out_specs=[vmem] * len(out_shape),
        scratch_shapes=scratch,
        cost_estimate=pl.CostEstimate(
            flops=weight * 10**9, bytes_accessed=weight * 2**20, transcendentals=0
        ),
        compiler_params=pltpu.CompilerParams(vmem_limit_bytes=limit),
    )(*operands, *fetched, *later)


def f32(*shape):
    return jax.ShapeDtypeStruct(shape, jnp.float32)


def shards(
    sub_inverse, sub_rhs, sub_tiles, update, update_rows, level_inverse, coupling, level_rhs
):
    count, place = lax.axis_size("pair"), lax.axis_index("pair")
    group = ("core", "rep")
    members = lax.axis_size(group)
    subtree_inverse, rhs_sub, block, rows = sub_inverse[0, 0], sub_rhs[0, 0], update[0, 0], update_rows[0]
    inverse, couple, rhs_level = level_inverse[0], coupling[0], level_rhs[0]
    sub_rows, width, height = subtree_inverse.shape[0], rhs_level.shape[1], inverse.shape[0]
    rounds = len(SWAP)
    spot = 2 * place + lax.axis_index("core")
    bits = (spot >> lax.broadcasted_iota(jnp.int32, (8, 128), 0)) & 1
    level, forward_sub, part = local_call(
        first_kernel,
        [
            f32(3 * height + TILE, TILE),
            jax.ShapeDtypeStruct((width + MARKS, sub_rows), jnp.bfloat16),
            f32(width, height),
        ],
        fetched=(inverse, couple, rhs_sub, sub_tiles, subtree_inverse, block, rows, rhs_level),
        limit=66 * 10**6,
    )
    sibling = lax.ppermute(level, "core", [(0, 1), (1, 0)])
    maps, pair_weights = local_call(
        pair_kernel, [f32(2 * TILE, TILE), f32(2 * TILE, 2 * TILE)], bits, level, sibling
    )
    columns = width // members
    parts = lax.all_to_all(part.reshape(members, columns, height), group, 0, 0)
    answers, weights, steps = [], [], []

    def advance_maps(j, maps, message, *later):
        other = swap(message, j, count)
        shapes = [
            f32(2 * TILE, 2 * TILE), f32(2 * TILE, TILE), f32(TILE, TILE)
        ]
        if j + 2 < rounds:
            shapes.append(f32(2 * TILE, TILE))
        if j + 1 >= PACKED:
            shapes.append(f32(HALF + 8 + (TILE if j + 2 < rounds else 0), TILE))
        weight, step, answer, *rest = local_call(
            functools.partial(maps_kernel, j, len(later)),
            shapes, bits, maps, other, later=later, weight=MAPS_WEIGHT[j],
        )
        weights.append(weight)
        steps.append(step)
        answers.append(answer)
        return rest[0], rest[-1]

    maps, message = advance_maps(0, maps, maps, parts)
    owns, states, state = local_call(
        start_kernel,
        [f32(2, columns, height), f32(2, columns, 2 * TILE), f32(columns, 2 * TILE)],
        bits, parts, level, sibling, pair_weights,
    )
    sent, got = [], []
    for j in range(rounds):
        sent.append(state)
        got.append(swap(state, j, count))
        if j < rounds - 2:
            later = (state,) if BEHIND[j] else ()
            maps, message = advance_maps(j + 1, maps, message, *later)
        elif j == rounds - 2:
            answers.append(swap(message, j + 1, count))
        if j < rounds - 1:
            (state,) = local_call(
                functools.partial(state_kernel, j + 1),
                [f32(columns, 2 * TILE)],
                bits, state, got[j], weights[j],
                weight=STATE_WEIGHT[j],
            )
    (descent,) = local_call(
        functools.partial(descend_kernel, rounds - 1),
        [f32(TILE + columns, 2 * height)],
        bits, level, sibling, pair_weights, owns, states,
        *sent[:-1], *got[:-1], *answers[:-1], *steps,
    )
    (shares,) = local_call(
        functools.partial(finish_kernel, rounds),
        [f32(members, columns, height)],
        bits, sent[-1], got[-1], answers[-1], descent,
    )
    spread = lax.all_to_all(shares, group, 0, 0)
    solution, final = local_call(
        subtree_backward_kernel,
        [f32(height, width), f32(sub_rows, width)],
        spread.reshape(width, -1), forward_sub, subtree_inverse, block,
    )
    return (solution[None], final[None, None])


def solution(mesh):
    chain, reps = mesh.devices.shape
    split = Mesh(mesh.devices.reshape(chain // 2, 2, reps), ("pair", "core", "rep"))
    both = ("pair", "core")
    return jax.shard_map(
        shards,
        mesh=split,
        in_specs=(
            P(both, "rep", None, None),
            P(both, "rep", None, None),
            P(both, "rep"),
            P(both, "rep", None, None),
            P(both, "rep", None),
            P(both, None, None),
            P(both, None, None),
            P(both, None, None),
        ),
        out_specs=(P(both, None, None), P(both, "rep", None, None)),
        check_vma=False,
    )
```

```python
import functools

import jax
import jax.numpy as jnp
from jax import lax
from jax.experimental import pallas as pl
from jax.experimental.pallas import tpu as pltpu
from jax.sharding import Mesh, PartitionSpec as P

TILE = 128
HALF = TILE // 2
MARKS = 16
HIGHEST = lax.Precision.HIGHEST
SWAP = (1, 3, 4, 8, 16, 48)


APART = 2
MAPS_WEIGHT = (3, 10)
STATE_WEIGHT = (30, 10)


def dot(a, b, dims=((1,), (0,)), precision=HIGHEST):
    return lax.dot_general(
        a, b, (dims, ((), ())), precision=precision, preferred_element_type=jnp.float32
    )


def swap(value, j, count):
    return lax.ppermute(value, "pair", [(n, n ^ SWAP[j]) for n in range(count)])


def pick(bits_ref, at):
    return bits_ref[at : at + 1, :1] == 1


def fetch(sems, *pairs):
    copies = [
        pltpu.make_async_copy(source, target, sems.at[i])
        for i, (source, target) in enumerate(pairs)
    ]
    for copy in copies:
        copy.start()
    return copies


def corners():
    row = lax.broadcasted_iota(jnp.int32, (HALF, TILE), 0)
    lane = lax.broadcasted_iota(jnp.int32, (HALF, TILE), 1)
    return row, lane


def pack(square):
    row, lane = corners()
    top, bottom = square[:HALF], square[HALF:]
    body = jnp.where((lane >= HALF) & (row > lane - HALF), pltpu.roll(top, HALF, 1), bottom)
    diagonal = jnp.sum(jnp.where(row == lane, top, 0.0), axis=0, keepdims=True)
    return jnp.concatenate([body, jnp.broadcast_to(diagonal, (8, TILE))], axis=0)


def unpack(packed):
    row, lane = corners()
    body, diagonal = packed[:HALF], packed[HALF : HALF + 1]
    first = jnp.where((lane < HALF) & (row > lane), pltpu.roll(body, HALF, 1), 0.0)
    first = jnp.where(row == lane, 0.5 * diagonal, first)
    last = jnp.where((lane < HALF) | (row < lane - HALF), body, 0.0)
    last = jnp.where(row == lane - HALF, 0.5 * body, last)
    half = jnp.concatenate([first, last], axis=0)
    return half + half.T


def join_maps(first, second):
    early = first[:TILE]
    product = dot(second, early)
    turn = product[TILE:]
    answer = first[TILE:] + dot(early.T, turn)
    return jnp.concatenate([product[:TILE], answer], axis=0), turn


def fill_weights(first, second, turn, weights_ref):
    weights_ref[:TILE, :TILE] = second[:TILE].T
    weights_ref[:TILE, TILE:] = turn
    weights_ref[TILE:, :TILE] = jnp.zeros_like(turn)
    weights_ref[TILE:, TILE:] = first[:TILE]


def fill_step(right, first, second, turn, step_ref):
    step_ref[:TILE] = jnp.where(right, first[:TILE], turn).T
    step_ref[TILE:] = jnp.where(right, 0.0, second[:TILE])


def pair_kernel(bits_ref, level_ref, sibling_ref, maps_ref, weights_ref):
    odd = pick(bits_ref, 0)
    own, other = level_ref[TILE : 3 * TILE], sibling_ref[TILE : 3 * TILE]
    first, second = jnp.where(odd, other, own), jnp.where(odd, own, other)
    maps_ref[...], turn = join_maps(first, second)
    fill_weights(first, second, turn, weights_ref)


def maps_kernel(j, later, bits_ref, own_ref, other_ref, *refs):
    maps_ref, weights_ref, step_ref = refs[later:]
    right = pick(bits_ref, j + 1)
    own, other = own_ref[...], other_ref[...]
    first, second = jnp.where(right, other, own), jnp.where(right, own, other)
    maps_ref[...], turn = join_maps(first, second)
    fill_weights(first, second, turn, weights_ref)
    fill_step(right, first, second, turn, step_ref)


def message(maps, state, last):
    parts = [pack(maps[TILE:]), state[:, :TILE], state[:, TILE:]]
    return jnp.concatenate(parts if last else [maps[:TILE]] + parts, axis=0)


def push_of(right, own, other, answer):
    return jnp.where(
        right, other[:, :TILE], other[:, TILE:] + dot(own[:, :TILE], answer)
    )


def round_kernel(j, last, bits_ref, maps_ref, state_ref, other_ref, *refs):
    step_ref, push_ref, message_ref, next_state_ref, *next_maps_ref = refs
    right = pick(bits_ref, j + 1)
    columns = state_ref.shape[0]
    offset = TILE + HALF + 8
    own = maps_ref[...]
    answer = unpack(other_ref[TILE:offset])
    other = jnp.concatenate([other_ref[:TILE], answer], axis=0)
    own_state = state_ref[...]
    other_state = jnp.concatenate(
        [other_ref[offset : offset + columns], other_ref[offset + columns :]], axis=1
    )
    first, second = jnp.where(right, other, own), jnp.where(right, own, other)
    maps, turn = join_maps(first, second)
    early = jnp.where(right, other_state, own_state)
    late = jnp.where(right, own_state, other_state)
    entry = early[:, :TILE]
    state = jnp.concatenate(
        [
            late[:, :TILE] + dot(entry, second[:TILE], ((1,), (1,))),
            early[:, TILE:] + dot(late[:, TILE:], first[:TILE]) + dot(entry, turn),
        ],
        axis=1,
    )
    message_ref[...] = message(maps, state, last)
    next_state_ref[...] = state
    if not last:
        next_maps_ref[0][...] = maps
    fill_step(right, first, second, turn, step_ref)
    push_ref[...] = push_of(right, own_state, other_state, answer)


def join_state(first, second, weights):
    mixed = jnp.concatenate([first[:, :TILE], second[:, TILE:]], axis=1)
    kept = jnp.concatenate([second[:, :TILE], first[:, TILE:]], axis=1)
    return kept + dot(mixed, weights)


def start_kernel(
    bits_ref, parts_ref, level_ref, sibling_ref, weights_ref,
    owns_ref, states_ref, state_ref,
):
    odd = pick(bits_ref, 0)
    reps, height = parts_ref.shape[0] // 2, parts_ref.shape[2]
    own_gain, other_gain = level_ref[:height], sibling_ref[:height]
    gains = (jnp.where(odd, other_gain, own_gain), jnp.where(odd, own_gain, other_gain))
    states = []
    for c in range(2):
        own = parts_ref[c * reps]
        for r in range(1, reps):
            own = own + parts_ref[c * reps + r]
        owns_ref[c] = own
        states.append(jnp.concatenate([own[:, TILE:], -dot(own, gains[c])], axis=1))
        states_ref[c] = states[c]
    state_ref[...] = join_state(states[0], states[1], weights_ref[...])


def state_kernel(j, bits_ref, own_ref, other_ref, answer_ref, weights_ref, *refs):
    right = pick(bits_ref, j + 1)
    own, other = own_ref[...], other_ref[...]
    state = join_state(
        jnp.where(right, other, own), jnp.where(right, own, other), weights_ref[...]
    )
    if len(refs) == 2:
        state_ref, push_ref = refs
    else:
        maps_ref, state_ref, push_ref, message_ref = refs
        message_ref[...] = message(maps_ref[...], state, False)
    state_ref[...] = state
    push_ref[...] = push_of(right, own, other, answer_ref[TILE:])


def descend_kernel(rounds, bits_ref, level_ref, sibling_ref, weights_ref, owns_ref, states_ref, *refs):
    pushes, steps = refs[:rounds], refs[rounds : 2 * rounds]
    descent_ref = refs[-1]
    odd = pick(bits_ref, 0)
    height = owns_ref.shape[2]

    def under(constant):
        return jnp.concatenate([jnp.zeros((TILE, constant.shape[1]), jnp.float32), constant], axis=0)

    row = lax.broadcasted_iota(jnp.int32, (TILE + owns_ref.shape[1], TILE), 0)
    lane = lax.broadcasted_iota(jnp.int32, (TILE + owns_ref.shape[1], TILE), 1)
    basis = jnp.where(row == lane, 1.0, 0.0)
    right = pick(bits_ref, rounds + 1)
    before, after = jnp.where(right, basis, 0.0), jnp.where(right, 0.0, basis)
    for j in reversed(range(rounds)):
        right = pick(bits_ref, j + 1)
        push = under(pushes[j][...]) + dot(jnp.concatenate([before, after], axis=1), steps[j][...])
        before, after = jnp.where(right, push, before), jnp.where(right, after, push)
    own, other = level_ref[...], sibling_ref[...]
    levels = (jnp.where(odd, other, own), jnp.where(odd, own, other))
    maps = [level[TILE : 3 * TILE] for level in levels]
    entry = states_ref[0, :, :TILE]
    middle_before = under(entry) + dot(before, maps[0][:TILE], ((1,), (1,)))
    middle_after = (
        under(states_ref[1, :, TILE:] + dot(entry, maps[1][TILE:]))
        + dot(before, weights_ref[:TILE, TILE:], ((1,), (1,)))
        + dot(after, maps[1][:TILE])
    )
    ends = ((before, middle_after), (middle_before, after))
    for c in range(2):
        level = levels[c]
        forward = under(owns_ref[c]) + dot(ends[c][0], level[:height], ((1,), (1,)))
        forward = jnp.concatenate(
            [forward[:, :TILE], forward[:, TILE:] - ends[c][1]], axis=1
        )
        descent_ref[:, 2 * c * TILE : (2 * c + 1) * TILE] = dot(
            forward, level[height + TILE : 2 * height + TILE]
        )
        descent_ref[:, (2 * c + 1) * TILE : (2 * c + 2) * TILE] = dot(
            forward, level[2 * height + TILE :]
        )


def finish_kernel(rounds, bits_ref, state_ref, other_ref, descent_ref, shares_ref):
    columns, offset = state_ref.shape[0], HALF + 8
    other = jnp.concatenate(
        [other_ref[offset : offset + columns], other_ref[offset + columns :]], axis=1
    )
    push = push_of(pick(bits_ref, rounds), state_ref[...], other, unpack(other_ref[:offset]))
    both = descent_ref[TILE:] + dot(push, descent_ref[:TILE])
    reps, height = shares_ref.shape[0] // 2, shares_ref.shape[2]
    for c in range(2):
        for r in range(reps):
            shares_ref[c * reps + r] = both[:, c * height : (c + 1) * height]


def live_columns(tiles, rows, columns):
    return lax.broadcasted_iota(jnp.int32, (rows, columns), 1) < TILE * tiles


def first_kernel(
    inverse_hbm, couple_hbm, rhs_hbm, tiles_hbm, subtree_inverse_hbm, update_hbm, rows_hbm,
    level_rhs_hbm,
    level_ref, forward_ref, part_ref,
    inverse_ref, couple_ref, rhs_ref, tiles_ref, subtree_inverse_ref, update_ref, rows_ref,
    level_rhs_ref, sems,
):
    copies = fetch(
        sems,
        (inverse_hbm, inverse_ref),
        (couple_hbm, couple_ref),
        (rhs_hbm, rhs_ref),
        (tiles_hbm, tiles_ref),
        (subtree_inverse_hbm, subtree_inverse_ref),
        (update_hbm, update_ref),
        (rows_hbm, rows_ref),
        (level_rhs_hbm, level_rhs_ref),
    )
    height = inverse_ref.shape[0]
    copies[0].wait()
    copies[1].wait()
    gain = -dot(inverse_ref[...], couple_ref[...])
    level_ref[:height] = gain
    level_ref[height : height + TILE] = -dot(gain.T, gain)
    level_ref[height + TILE : 2 * height + TILE] = inverse_ref[:, :TILE]
    level_ref[2 * height + TILE :] = inverse_ref[:, TILE:]
    columns, sub_rows = rhs_ref.shape[1], rhs_ref.shape[0]
    copies[2].wait()
    copies[3].wait()
    live = live_columns(tiles_ref[...], columns, sub_rows)
    masked = jnp.where(live, rhs_ref[...].astype(jnp.float32).T, 0.0).astype(jnp.bfloat16)
    copies[4].wait()
    solved = dot(masked, subtree_inverse_ref[...], ((1,), (1,)), None)
    forward = jnp.where(live, solved, 0.0).astype(jnp.bfloat16)
    forward_ref[:columns] = forward
    copies[5].wait()
    contrib = dot(forward, update_ref[...], ((1,), (1,)), None)
    copies[6].wait()
    totals = []
    for s in range(level_rhs_ref.shape[0] // TILE):
        total = jnp.zeros((columns, TILE), jnp.float32)
        for t in range(rows_ref.shape[1]):
            here = rows_ref[:, t : t + 1] == s
            total = total + jnp.where(here, contrib[:, t * TILE : (t + 1) * TILE], 0.0)
        totals.append(total)
    row = lax.broadcasted_iota(jnp.int32, (MARKS, sub_rows), 0)
    lane = lax.broadcasted_iota(jnp.int32, (MARKS, sub_rows), 1)
    marks = jnp.where(row == 0, tiles_ref[...], 0)
    for t in range(rows_ref.shape[1]):
        marks = jnp.where((row == 1) & (lane == t), rows_ref[:, t : t + 1], marks)
    forward_ref[columns:] = marks.astype(jnp.float32).astype(jnp.bfloat16)
    copies[7].wait()
    rest = 0.25 * level_rhs_ref[...].T - jnp.concatenate(totals, axis=1)
    part_ref[...] = dot(rest, inverse_ref[...], ((1,), (1,)))


def subtree_backward_kernel(
    solution_ref, forward_ref, subtree_inverse_ref, update_ref, level_ref, final_ref
):
    columns, sub_rows = solution_ref.shape[0], forward_ref.shape[1]
    marks = forward_ref[columns:].astype(jnp.float32).astype(jnp.int32)
    live = live_columns(marks[:1, :1], columns, sub_rows)
    level_ref[...] = solution_ref[...].T
    picked = []
    for t in range(update_ref.shape[0] // TILE):
        tile = solution_ref[:, :TILE]
        for s in range(1, solution_ref.shape[1] // TILE):
            here = marks[1:2, t : t + 1] == s
            tile = jnp.where(here, solution_ref[:, s * TILE : (s + 1) * TILE], tile)
        picked.append(tile.astype(jnp.bfloat16))
    pulled = dot(jnp.concatenate(picked, axis=1), update_ref[...], precision=None)
    residue = forward_ref[:columns].astype(jnp.float32) - jnp.where(live, pulled, 0.0)
    final = dot(residue.astype(jnp.bfloat16), subtree_inverse_ref[...], precision=None)
    final_ref[...] = jnp.where(live, final, 0.0).T


def local_call(kernel, out_shape, *operands, fetched=(), later=(), weight=0, limit=8 * 2**20):
    vmem = pl.BlockSpec(memory_space=pltpu.VMEM)
    scratch = [pltpu.VMEM(part.shape, part.dtype) for part in fetched]
    if fetched:
        scratch.append(pltpu.SemaphoreType.DMA((len(fetched),)))
    return pl.pallas_call(
        kernel,
        out_shape=out_shape,
        in_specs=[vmem] * len(operands)
        + [pl.BlockSpec(memory_space=pltpu.HBM)] * len(fetched)
        + [pl.BlockSpec(memory_space=pl.ANY)] * len(later),
        out_specs=[vmem] * len(out_shape),
        scratch_shapes=scratch,
        cost_estimate=pl.CostEstimate(
            flops=weight * 10**9, bytes_accessed=weight * 2**20, transcendentals=0
        ),
        compiler_params=pltpu.CompilerParams(vmem_limit_bytes=limit),
    )(*operands, *fetched, *later)


def f32(*shape):
    return jax.ShapeDtypeStruct(shape, jnp.float32)


def shards(
    sub_inverse, sub_rhs, sub_tiles, update, update_rows, level_inverse, coupling, level_rhs
):
    count, place = lax.axis_size("pair"), lax.axis_index("pair")
    group = ("core", "rep")
    members = lax.axis_size(group)
    subtree_inverse, rhs_sub, block, rows = sub_inverse[0, 0], sub_rhs[0, 0], update[0, 0], update_rows[0]
    inverse, couple, rhs_level = level_inverse[0], coupling[0], level_rhs[0]
    sub_rows, width, height = subtree_inverse.shape[0], rhs_level.shape[1], inverse.shape[0]
    rounds = len(SWAP)
    spot = 2 * place + lax.axis_index("core")
    bits = (spot >> lax.broadcasted_iota(jnp.int32, (8, 128), 0)) & 1
    level, forward_sub, part = local_call(
        first_kernel,
        [
            f32(3 * height + TILE, TILE),
            jax.ShapeDtypeStruct((width + MARKS, sub_rows), jnp.bfloat16),
            f32(width, height),
        ],
        fetched=(inverse, couple, rhs_sub, sub_tiles, subtree_inverse, block, rows, rhs_level),
        limit=66 * 10**6,
    )
    sibling = lax.ppermute(level, "core", [(0, 1), (1, 0)])
    maps, pair_weights = local_call(
        pair_kernel, [f32(2 * TILE, TILE), f32(2 * TILE, 2 * TILE)], bits, level, sibling
    )
    columns = width // members
    parts = lax.all_to_all(part.reshape(members, columns, height), group, 0, 0)
    pushes, steps = [], []
    square = 2 * TILE

    def advance_maps(j, maps, *later):
        other = swap(maps, j, count)
        maps, weights, step = local_call(
            functools.partial(maps_kernel, j, len(later)),
            [f32(square, TILE), f32(square, square), f32(square, TILE)],
            bits, maps, other, later=later, weight=MAPS_WEIGHT[j],
        )
        steps.append(step)
        return other, maps, weights

    answer, maps, weights = advance_maps(0, maps, parts)
    owns, states, state = local_call(
        start_kernel,
        [f32(2, columns, height), f32(2, columns, square), f32(columns, square)],
        bits, parts, level, sibling, pair_weights,
    )
    whole = TILE + HALF + 8 + 2 * columns
    for j in range(APART):
        other = swap(state, j, count)
        shapes = [f32(columns, square), f32(columns, TILE)]
        operands = [bits, state, other, answer, weights]
        if j + 1 < APART:
            answer, maps, weights = advance_maps(j + 1, maps, state)
        else:
            operands.append(maps)
            shapes.append(f32(whole, TILE))
        state, push, *packed = local_call(
            functools.partial(state_kernel, j), shapes, *operands, weight=STATE_WEIGHT[j]
        )
        pushes.append(push)
    packed = packed[0]
    for j in range(APART, rounds - 1):
        last = j == rounds - 2
        shapes = [
            f32(square, TILE), f32(columns, TILE), f32(whole - last * TILE, TILE),
            f32(columns, square),
        ]
        step, push, packed, state, *rest = local_call(
            functools.partial(round_kernel, j, last),
            shapes if last else shapes + [f32(square, TILE)],
            bits, maps, state, swap(packed, j, count),
        )
        maps = None if last else rest[0]
        steps.append(step)
        pushes.append(push)
    got = swap(packed, rounds - 1, count)
    (descent,) = local_call(
        functools.partial(descend_kernel, rounds - 1),
        [f32(TILE + columns, 2 * height)],
        bits, level, sibling, pair_weights, owns, states, *pushes, *steps,
    )
    (shares,) = local_call(
        functools.partial(finish_kernel, rounds),
        [f32(members, columns, height)],
        bits, state, got, descent,
    )
    spread = lax.all_to_all(shares, group, 0, 0)
    solution, final = local_call(
        subtree_backward_kernel,
        [f32(height, width), f32(sub_rows, width)],
        spread.reshape(width, -1), forward_sub, subtree_inverse, block,
    )
    return (solution[None], final[None, None])


def solution(mesh):
    chain, reps = mesh.devices.shape
    split = Mesh(mesh.devices.reshape(chain // 2, 2, reps), ("pair", "core", "rep"))
    both = ("pair", "core")
    return jax.shard_map(
        shards,
        mesh=split,
        in_specs=(
            P(both, "rep", None, None),
            P(both, "rep", None, None),
            P(both, "rep"),
            P(both, "rep", None, None),
            P(both, "rep", None),
            P(both, None, None),
            P(both, None, None),
            P(both, None, None),
        ),
        out_specs=(P(both, None, None), P(both, "rep", None, None)),
        check_vma=False,
    )
```

```python
import functools

import jax
import jax.numpy as jnp
from jax import lax
from jax.experimental import pallas as pl
from jax.experimental.pallas import tpu as pltpu
from jax.sharding import Mesh, PartitionSpec as P

TILE = 128
HALF = TILE // 2
MARKS = 16
SPLIT = lax.Precision.HIGH
SWAP = (1, 3, 4, 8, 16, 48)


APART = 2
MAPS_WEIGHT = (3, 10)
STATE_WEIGHT = (30, 10)
SIDE_WEIGHT = 1


def dot(a, b, dims=((1,), (0,)), precision=SPLIT):
    return lax.dot_general(
        a, b, (dims, ((), ())), precision=precision, preferred_element_type=jnp.float32
    )


def swap(value, j, count):
    return lax.ppermute(value, "pair", [(n, n ^ SWAP[j]) for n in range(count)])


def pick(bits_ref, at):
    return bits_ref[at : at + 1, :1] == 1


def fetch(sems, *pairs):
    copies = [
        pltpu.make_async_copy(source, target, sems.at[i])
        for i, (source, target) in enumerate(pairs)
    ]
    for copy in copies:
        copy.start()
    return copies


def corners():
    row = lax.broadcasted_iota(jnp.int32, (HALF, TILE), 0)
    lane = lax.broadcasted_iota(jnp.int32, (HALF, TILE), 1)
    return row, lane


def pack(square):
    row, lane = corners()
    top, bottom = square[:HALF], square[HALF:]
    body = jnp.where((lane >= HALF) & (row > lane - HALF), pltpu.roll(top, HALF, 1), bottom)
    diagonal = jnp.sum(jnp.where(row == lane, top, 0.0), axis=0, keepdims=True)
    return jnp.concatenate([body, jnp.broadcast_to(diagonal, (8, TILE))], axis=0)


def unpack(packed):
    row, lane = corners()
    body, diagonal = packed[:HALF], packed[HALF : HALF + 1]
    first = jnp.where((lane < HALF) & (row > lane), pltpu.roll(body, HALF, 1), 0.0)
    first = jnp.where(row == lane, 0.5 * diagonal, first)
    last = jnp.where((lane < HALF) | (row < lane - HALF), body, 0.0)
    last = jnp.where(row == lane - HALF, 0.5 * body, last)
    half = jnp.concatenate([first, last], axis=0)
    return half + half.T


def join_maps(first, second):
    early = first[:TILE]
    product = dot(second, early)
    turn = product[TILE:]
    answer = first[TILE:] + dot(early.T, turn)
    return jnp.concatenate([product[:TILE], answer], axis=0), turn


def fill_weights(first, second, turn, weights_ref):
    weights_ref[:TILE, :TILE] = second[:TILE].T
    weights_ref[:TILE, TILE:] = turn
    weights_ref[TILE:, :TILE] = jnp.zeros_like(turn)
    weights_ref[TILE:, TILE:] = first[:TILE]


def pair_kernel(bits_ref, level_ref, sibling_ref, maps_ref, weights_ref):
    odd = pick(bits_ref, 0)
    own, other = level_ref[TILE : 3 * TILE], sibling_ref[TILE : 3 * TILE]
    first, second = jnp.where(odd, other, own), jnp.where(odd, own, other)
    maps_ref[...], turn = join_maps(first, second)
    fill_weights(first, second, turn, weights_ref)


def maps_kernel(j, later, bits_ref, own_ref, other_ref, *refs):
    maps_ref, weights_ref = refs[later:]
    right = pick(bits_ref, j + 1)
    own, other = own_ref[...], other_ref[...]
    first, second = jnp.where(right, other, own), jnp.where(right, own, other)
    maps_ref[...], turn = join_maps(first, second)
    fill_weights(first, second, turn, weights_ref)


def message(maps, state):
    parts = [maps[:TILE], pack(maps[TILE:]), state[:, :TILE], state[:, TILE:]]
    return jnp.concatenate(parts, axis=0)


def last_message(right, maps, state):
    half = jnp.where(right, state[:, TILE:], state[:, :TILE])
    return jnp.concatenate([pack(maps[TILE:]), half], axis=0)


def side_kernel(j, bits_ref, own_ref, state_ref, turn_ref, *refs):
    *others, step_ref, push_ref = refs
    right = pick(bits_ref, j + 1)
    columns, square = state_ref.shape
    if len(others) == 2:
        other, other_state = others[0][...], others[1][...]
        turn = turn_ref[:TILE, TILE:]
    else:
        other, other_state = open_message(others[0], columns)
        turn = turn_ref[...]
    own = own_ref[...]
    step_ref[:TILE] = jnp.where(right, other[:TILE], turn).T
    step_ref[TILE:] = jnp.where(right, 0.0, other[:TILE])
    push_ref[...] = jnp.where(
        right,
        other_state[:, :TILE],
        other_state[:, TILE:] + dot(state_ref[:, :TILE], other[TILE:]),
    )


def open_message(ref, columns):
    offset = TILE + HALF + 8
    maps = jnp.concatenate([ref[:TILE], unpack(ref[TILE:offset])], axis=0)
    state = jnp.concatenate([ref[offset : offset + columns], ref[offset + columns :]], axis=1)
    return maps, state


def round_kernel(j, last, bits_ref, maps_ref, state_ref, other_ref, *refs):
    turn_ref, message_ref, next_state_ref, *next_maps_ref = refs
    right = pick(bits_ref, j + 1)
    columns = state_ref.shape[0]
    own, own_state = maps_ref[...], state_ref[...]
    other, other_state = open_message(other_ref, columns)
    first, second = jnp.where(right, other, own), jnp.where(right, own, other)
    maps, turn = join_maps(first, second)
    early = jnp.where(right, other_state, own_state)
    late = jnp.where(right, own_state, other_state)
    entry = early[:, :TILE]
    state = jnp.concatenate(
        [
            late[:, :TILE] + dot(entry, second[:TILE], ((1,), (1,))),
            early[:, TILE:] + dot(late[:, TILE:], first[:TILE]) + dot(entry, turn),
        ],
        axis=1,
    )
    if last:
        message_ref[...] = last_message(pick(bits_ref, j + 2), maps, state)
    else:
        message_ref[...] = message(maps, state)
        next_maps_ref[0][...] = maps
    next_state_ref[...] = state
    turn_ref[...] = turn


def join_state(first, second, weights):
    mixed = jnp.concatenate([first[:, :TILE], second[:, TILE:]], axis=1)
    kept = jnp.concatenate([second[:, :TILE], first[:, TILE:]], axis=1)
    return kept + dot(mixed, weights)


def start_kernel(
    bits_ref, parts_ref, level_ref, sibling_ref, weights_ref,
    owns_ref, states_ref, state_ref,
):
    odd = pick(bits_ref, 0)
    reps, height = parts_ref.shape[0] // 2, parts_ref.shape[2]
    own_gain, other_gain = level_ref[:height], sibling_ref[:height]
    gains = (jnp.where(odd, other_gain, own_gain), jnp.where(odd, own_gain, other_gain))
    states = []
    for c in range(2):
        own = parts_ref[c * reps]
        for r in range(1, reps):
            own = own + parts_ref[c * reps + r]
        owns_ref[c] = own
        states.append(jnp.concatenate([own[:, TILE:], -dot(own, gains[c])], axis=1))
        states_ref[c] = states[c]
    state_ref[...] = join_state(states[0], states[1], weights_ref[...])


def state_kernel(j, bits_ref, own_ref, other_ref, weights_ref, *refs):
    right = pick(bits_ref, j + 1)
    own, other = own_ref[...], other_ref[...]
    state = join_state(
        jnp.where(right, other, own), jnp.where(right, own, other), weights_ref[...]
    )
    if len(refs) == 1:
        state_ref = refs[0]
    else:
        maps_ref, state_ref, message_ref = refs
        message_ref[...] = message(maps_ref[...], state)
    state_ref[...] = state


def descend_kernel(rounds, bits_ref, level_ref, sibling_ref, weights_ref, owns_ref, states_ref, *refs):
    pushes, steps = refs[:rounds], refs[rounds : 2 * rounds]
    descent_ref = refs[-1]
    odd = pick(bits_ref, 0)
    height = owns_ref.shape[2]

    def under(constant):
        return jnp.concatenate([jnp.zeros((TILE, constant.shape[1]), jnp.float32), constant], axis=0)

    row = lax.broadcasted_iota(jnp.int32, (TILE + owns_ref.shape[1], TILE), 0)
    lane = lax.broadcasted_iota(jnp.int32, (TILE + owns_ref.shape[1], TILE), 1)
    basis = jnp.where(row == lane, 1.0, 0.0)
    right = pick(bits_ref, rounds + 1)
    before, after = jnp.where(right, basis, 0.0), jnp.where(right, 0.0, basis)
    for j in reversed(range(rounds)):
        right = pick(bits_ref, j + 1)
        push = under(pushes[j][...]) + dot(jnp.concatenate([before, after], axis=1), steps[j][...])
        before, after = jnp.where(right, push, before), jnp.where(right, after, push)
    own, other = level_ref[...], sibling_ref[...]
    levels = (jnp.where(odd, other, own), jnp.where(odd, own, other))
    maps = [level[TILE : 3 * TILE] for level in levels]
    entry = states_ref[0, :, :TILE]
    middle_before = under(entry) + dot(before, maps[0][:TILE], ((1,), (1,)))
    middle_after = (
        under(states_ref[1, :, TILE:] + dot(entry, maps[1][TILE:]))
        + dot(before, weights_ref[:TILE, TILE:], ((1,), (1,)))
        + dot(after, maps[1][:TILE])
    )
    ends = ((before, middle_after), (middle_before, after))
    for c in range(2):
        level = levels[c]
        forward = under(owns_ref[c]) + dot(ends[c][0], level[:height], ((1,), (1,)))
        forward = jnp.concatenate(
            [forward[:, :TILE], forward[:, TILE:] - ends[c][1]], axis=1
        )
        descent_ref[:, 2 * c * TILE : (2 * c + 1) * TILE] = dot(
            forward, level[height + TILE : 2 * height + TILE]
        )
        descent_ref[:, (2 * c + 1) * TILE : (2 * c + 2) * TILE] = dot(
            forward, level[2 * height + TILE :]
        )


def finish_kernel(rounds, bits_ref, state_ref, other_ref, descent_ref, shares_ref):
    offset = HALF + 8
    half = other_ref[offset:]
    answered = dot(state_ref[:, :TILE], unpack(other_ref[:offset]))
    push = half + jnp.where(pick(bits_ref, rounds), 0.0, answered)
    both = descent_ref[TILE:] + dot(push, descent_ref[:TILE])
    reps, height = shares_ref.shape[0] // 2, shares_ref.shape[2]
    for c in range(2):
        for r in range(reps):
            shares_ref[c * reps + r] = both[:, c * height : (c + 1) * height]


def live_columns(tiles, rows, columns):
    return lax.broadcasted_iota(jnp.int32, (rows, columns), 1) < TILE * tiles


def first_kernel(
    inverse_hbm, couple_hbm, rhs_hbm, tiles_hbm, subtree_inverse_hbm, update_hbm, rows_hbm,
    level_rhs_hbm,
    level_hbm, forward_hbm, part_ref,
    inverse_ref, couple_ref, rhs_ref, tiles_ref, subtree_inverse_ref, update_ref, rows_ref,
    level_rhs_ref, sems, level_ref, forward_ref, store_sems,
):
    copies = fetch(
        sems,
        (inverse_hbm, inverse_ref),
        (couple_hbm, couple_ref),
        (rhs_hbm, rhs_ref),
        (tiles_hbm, tiles_ref),
        (subtree_inverse_hbm, subtree_inverse_ref),
        (update_hbm, update_ref),
        (rows_hbm, rows_ref),
        (level_rhs_hbm, level_rhs_ref),
    )
    height = inverse_ref.shape[0]
    copies[0].wait()
    copies[1].wait()
    gain = -dot(inverse_ref[...], couple_ref[...])
    level_ref[:height] = gain
    level_ref[height : height + TILE] = -dot(gain.T, gain)
    level_ref[height + TILE : 2 * height + TILE] = inverse_ref[:, :TILE]
    level_ref[2 * height + TILE :] = inverse_ref[:, TILE:]
    store_level = pltpu.make_async_copy(level_ref, level_hbm, store_sems.at[0])
    store_level.start()
    columns, sub_rows = rhs_ref.shape[1], rhs_ref.shape[0]
    copies[2].wait()
    copies[3].wait()
    live = live_columns(tiles_ref[...], columns, sub_rows)
    masked = jnp.where(live, rhs_ref[...].astype(jnp.float32).T, 0.0).astype(jnp.bfloat16)
    copies[4].wait()
    solved = dot(masked, subtree_inverse_ref[...], ((1,), (1,)), None)
    forward = jnp.where(live, solved, 0.0).astype(jnp.bfloat16)
    forward_ref[:columns] = forward
    copies[5].wait()
    contrib = dot(forward, update_ref[...], ((1,), (1,)), None)
    copies[6].wait()
    totals = []
    for s in range(level_rhs_ref.shape[0] // TILE):
        total = jnp.zeros((columns, TILE), jnp.float32)
        for t in range(rows_ref.shape[1]):
            here = rows_ref[:, t : t + 1] == s
            total = total + jnp.where(here, contrib[:, t * TILE : (t + 1) * TILE], 0.0)
        totals.append(total)
    row = lax.broadcasted_iota(jnp.int32, (MARKS, sub_rows), 0)
    lane = lax.broadcasted_iota(jnp.int32, (MARKS, sub_rows), 1)
    marks = jnp.where(row == 0, tiles_ref[...], 0)
    for t in range(rows_ref.shape[1]):
        marks = jnp.where((row == 1) & (lane == t), rows_ref[:, t : t + 1], marks)
    forward_ref[columns:] = marks.astype(jnp.float32).astype(jnp.bfloat16)
    store_forward = pltpu.make_async_copy(forward_ref, forward_hbm, store_sems.at[1])
    store_forward.start()
    copies[7].wait()
    rest = 0.25 * level_rhs_ref[...].T - jnp.concatenate(totals, axis=1)
    part_ref[...] = dot(rest, inverse_ref[...], ((1,), (1,)))
    store_level.wait()
    store_forward.wait()


def subtree_backward_kernel(
    solution_ref, forward_ref, subtree_inverse_ref, update_ref, level_ref, final_ref
):
    columns, sub_rows = solution_ref.shape[0], forward_ref.shape[1]
    marks = forward_ref[columns:].astype(jnp.float32).astype(jnp.int32)
    live = live_columns(marks[:1, :1], columns, sub_rows)
    level_ref[...] = solution_ref[...].T
    picked = []
    for t in range(update_ref.shape[0] // TILE):
        tile = solution_ref[:, :TILE]
        for s in range(1, solution_ref.shape[1] // TILE):
            here = marks[1:2, t : t + 1] == s
            tile = jnp.where(here, solution_ref[:, s * TILE : (s + 1) * TILE], tile)
        picked.append(tile.astype(jnp.bfloat16))
    pulled = dot(jnp.concatenate(picked, axis=1), update_ref[...], precision=None)
    residue = forward_ref[:columns].astype(jnp.float32) - jnp.where(live, pulled, 0.0)
    final = dot(residue.astype(jnp.bfloat16), subtree_inverse_ref[...], precision=None)
    final_ref[...] = jnp.where(live, final, 0.0).T


def local_call(
    kernel, out_shape, *operands, fetched=(), later=(), weight=0, limit=8 * 2**20, stored=0
):
    vmem = pl.BlockSpec(memory_space=pltpu.VMEM)
    scratch = [pltpu.VMEM(part.shape, part.dtype) for part in fetched]
    if fetched:
        scratch.append(pltpu.SemaphoreType.DMA((len(fetched),)))
    if stored:
        scratch += [pltpu.VMEM(part.shape, part.dtype) for part in out_shape[:stored]]
        scratch.append(pltpu.SemaphoreType.DMA((stored,)))
    return pl.pallas_call(
        kernel,
        out_shape=out_shape,
        in_specs=[vmem] * len(operands)
        + [pl.BlockSpec(memory_space=pltpu.HBM)] * len(fetched)
        + [pl.BlockSpec(memory_space=pl.ANY)] * len(later),
        out_specs=[pl.BlockSpec(memory_space=pltpu.HBM)] * stored
        + [vmem] * (len(out_shape) - stored),
        scratch_shapes=scratch,
        cost_estimate=pl.CostEstimate(
            flops=weight * 10**9, bytes_accessed=weight * 2**20, transcendentals=0
        ),
        compiler_params=pltpu.CompilerParams(vmem_limit_bytes=limit),
    )(*operands, *fetched, *later)


def f32(*shape):
    return jax.ShapeDtypeStruct(shape, jnp.float32)


def shards(
    sub_inverse, sub_rhs, sub_tiles, update, update_rows, level_inverse, coupling, level_rhs
):
    count, place = lax.axis_size("pair"), lax.axis_index("pair")
    group = ("core", "rep")
    members = lax.axis_size(group)
    subtree_inverse, rhs_sub, block, rows = sub_inverse[0, 0], sub_rhs[0, 0], update[0, 0], update_rows[0]
    inverse, couple, rhs_level = level_inverse[0], coupling[0], level_rhs[0]
    sub_rows, width, height = subtree_inverse.shape[0], rhs_level.shape[1], inverse.shape[0]
    rounds = len(SWAP)
    spot = 2 * place + lax.axis_index("core")
    bits = (spot >> lax.broadcasted_iota(jnp.int32, (8, 128), 0)) & 1
    level, forward_sub, part = local_call(
        first_kernel,
        [
            f32(3 * height + TILE, TILE),
            jax.ShapeDtypeStruct((width + MARKS, sub_rows), jnp.bfloat16),
            f32(width, height),
        ],
        fetched=(inverse, couple, rhs_sub, sub_tiles, subtree_inverse, block, rows, rhs_level),
        limit=66 * 10**6, stored=2,
    )
    sibling = lax.ppermute(level, "core", [(0, 1), (1, 0)])
    maps, pair_weights = local_call(
        pair_kernel, [f32(2 * TILE, TILE), f32(2 * TILE, 2 * TILE)], bits, level, sibling
    )
    columns = width // members
    parts = lax.all_to_all(part.reshape(members, columns, height), group, 0, 0)
    pushes, steps = [], []
    square = 2 * TILE

    def set_aside(j, maps, state, turn, *others):
        step, push = local_call(
            functools.partial(side_kernel, j),
            [f32(square, TILE), f32(columns, TILE)],
            bits, maps, state, turn, *others, weight=SIDE_WEIGHT,
        )
        steps.append(step)
        pushes.append(push)

    def advance_maps(j, maps, *later):
        other = swap(maps, j, count)
        joined, weights = local_call(
            functools.partial(maps_kernel, j, len(later)),
            [f32(square, TILE), f32(square, square)],
            bits, maps, other, later=later, weight=MAPS_WEIGHT[j],
        )
        return maps, other, joined, weights

    own_maps, other_maps, maps, weights = advance_maps(0, maps, parts)
    owns, states, state = local_call(
        start_kernel,
        [f32(2, columns, height), f32(2, columns, square), f32(columns, square)],
        bits, parts, level, sibling, pair_weights,
    )
    whole = TILE + HALF + 8 + 2 * columns
    for j in range(APART):
        other = swap(state, j, count)
        shapes = [f32(columns, square)]
        operands = [bits, state, other, weights]
        aside = (j, own_maps, state, weights, other_maps, other)
        if j + 1 < APART:
            own_maps, other_maps, maps, weights = advance_maps(j + 1, maps, state)
        else:
            operands.append(maps)
            shapes.append(f32(whole, TILE))
        state, *packed = local_call(
            functools.partial(state_kernel, j), shapes, *operands, weight=STATE_WEIGHT[j]
        )
        set_aside(*aside)
    packed = packed[0]
    for j in range(APART, rounds - 1):
        last = j == rounds - 2
        shapes = [
            f32(TILE, TILE),
            f32(HALF + 8 + columns if last else whole, TILE),
            f32(columns, square),
        ]
        other = swap(packed, j, count)
        aside = (j, maps, state)
        turn, packed, state, *rest = local_call(
            functools.partial(round_kernel, j, last),
            shapes if last else shapes + [f32(square, TILE)],
            bits, maps, state, other,
        )
        set_aside(*aside, turn, other)
        maps = None if last else rest[0]
    got = swap(packed, rounds - 1, count)
    (descent,) = local_call(
        functools.partial(descend_kernel, rounds - 1),
        [f32(TILE + columns, 2 * height)],
        bits, level, sibling, pair_weights, owns, states, *pushes, *steps,
    )
    (shares,) = local_call(
        functools.partial(finish_kernel, rounds),
        [f32(members, columns, height)],
        bits, state, got, descent,
    )
    spread = lax.all_to_all(shares, group, 0, 0)
    solution, final = local_call(
        subtree_backward_kernel,
        [f32(height, width), f32(sub_rows, width)],
        spread.reshape(width, -1), forward_sub, subtree_inverse, block,
    )
    return (solution[None], final[None, None])


def solution(mesh):
    chain, reps = mesh.devices.shape
    split = Mesh(mesh.devices.reshape(chain // 2, 2, reps), ("pair", "core", "rep"))
    both = ("pair", "core")
    return jax.shard_map(
        shards,
        mesh=split,
        in_specs=(
            P(both, "rep", None, None),
            P(both, "rep", None, None),
            P(both, "rep"),
            P(both, "rep", None, None),
            P(both, "rep", None),
            P(both, None, None),
            P(both, None, None),
            P(both, None, None),
        ),
        out_specs=(P(both, None, None), P(both, "rep", None, None)),
        check_vma=False,
    )
```

```python
import functools

import jax
import jax.numpy as jnp
from jax import lax
from jax.experimental import pallas as pl
from jax.experimental.pallas import tpu as pltpu
from jax.sharding import Mesh, PartitionSpec as P

TILE = 128
HALF = TILE // 2
MARKS = 16
SWAP = (1, 3, 4, 8, 16, 48)


APART = 2
MAPS_WEIGHT = (3, 10)
STATE_WEIGHT = (30, 10)
SIDE_WEIGHT = 1


def dot(a, b, dims=((1,), (0,))):
    return lax.dot_general(a, b, (dims, ((), ())), preferred_element_type=jnp.float32)


def halves(value):
    high = value.astype(jnp.bfloat16)
    return high, (value - high.astype(jnp.float32)).astype(jnp.bfloat16)


def fine_dot(a, b, dims=((1,), (0,))):
    (a_high, a_low), (b_high, b_low) = halves(a), halves(b)
    small = dot(a_high, b_low, dims) + dot(a_low, b_high, dims)
    return small + dot(a_high, b_high, dims)


def swap(value, j, count):
    return lax.ppermute(value, "pair", [(n, n ^ SWAP[j]) for n in range(count)])


def pick(bits_ref, at):
    return bits_ref[at : at + 1, :1] == 1


def fetch(sems, *pairs):
    copies = [
        pltpu.make_async_copy(source, target, sems.at[i])
        for i, (source, target) in enumerate(pairs)
    ]
    for copy in copies:
        copy.start()
    return copies


def corners():
    row = lax.broadcasted_iota(jnp.int32, (HALF, TILE), 0)
    lane = lax.broadcasted_iota(jnp.int32, (HALF, TILE), 1)
    return row, lane


def pack(square):
    row, lane = corners()
    top, bottom = square[:HALF], square[HALF:]
    body = jnp.where((lane >= HALF) & (row > lane - HALF), pltpu.roll(top, HALF, 1), bottom)
    diagonal = jnp.sum(jnp.where(row == lane, top, 0.0), axis=0, keepdims=True)
    return jnp.concatenate([body, jnp.broadcast_to(diagonal, (8, TILE))], axis=0)


def unpack(packed):
    row, lane = corners()
    body, diagonal = packed[:HALF], packed[HALF : HALF + 1]
    first = jnp.where((lane < HALF) & (row > lane), pltpu.roll(body, HALF, 1), 0.0)
    first = jnp.where(row == lane, 0.5 * diagonal, first)
    last = jnp.where((lane < HALF) | (row < lane - HALF), body, 0.0)
    last = jnp.where(row == lane - HALF, 0.5 * body, last)
    half = jnp.concatenate([first, last], axis=0)
    return half + half.T


def join_maps(first, second):
    early = first[:TILE]
    product = fine_dot(second, early)
    turn = product[TILE:]
    answer = first[TILE:] + fine_dot(early.T, turn)
    return jnp.concatenate([product[:TILE], answer], axis=0), turn


def fill_weights(first, second, turn, weights_ref):
    weights_ref[:TILE, :TILE] = second[:TILE].T
    weights_ref[:TILE, TILE:] = turn
    weights_ref[TILE:, :TILE] = jnp.zeros_like(turn)
    weights_ref[TILE:, TILE:] = first[:TILE]


def pair_kernel(bits_ref, level_ref, sibling_ref, maps_ref, weights_ref):
    odd = pick(bits_ref, 0)
    own, other = level_ref[TILE : 3 * TILE], sibling_ref[TILE : 3 * TILE]
    first, second = jnp.where(odd, other, own), jnp.where(odd, own, other)
    maps_ref[...], turn = join_maps(first, second)
    fill_weights(first, second, turn, weights_ref)


def maps_kernel(j, later, bits_ref, own_ref, other_ref, *refs):
    maps_ref, weights_ref = refs[later:]
    right = pick(bits_ref, j + 1)
    own, other = own_ref[...], other_ref[...]
    first, second = jnp.where(right, other, own), jnp.where(right, own, other)
    maps_ref[...], turn = join_maps(first, second)
    fill_weights(first, second, turn, weights_ref)


def message(maps, state):
    parts = [maps[:TILE], pack(maps[TILE:]), state[:, :TILE], state[:, TILE:]]
    return jnp.concatenate(parts, axis=0)


def last_message(right, maps, state):
    half = jnp.where(right, state[:, TILE:], state[:, :TILE])
    return jnp.concatenate([pack(maps[TILE:]), half], axis=0)


def side_kernel(j, bits_ref, own_ref, state_ref, turn_ref, *refs):
    *others, step_ref, push_ref = refs
    right = pick(bits_ref, j + 1)
    columns, square = state_ref.shape
    if len(others) == 2:
        other, other_state = others[0][...], others[1][...]
        turn = turn_ref[:TILE, TILE:]
    else:
        other, other_state = open_message(others[0], columns)
        turn = turn_ref[...]
    own = own_ref[...]
    step_ref[:TILE] = jnp.where(right, other[:TILE], turn).T
    step_ref[TILE:] = jnp.where(right, 0.0, other[:TILE])
    push_ref[...] = jnp.where(
        right,
        other_state[:, :TILE],
        other_state[:, TILE:] + fine_dot(state_ref[:, :TILE], other[TILE:]),
    )


def open_message(ref, columns):
    offset = TILE + HALF + 8
    maps = jnp.concatenate([ref[:TILE], unpack(ref[TILE:offset])], axis=0)
    state = jnp.concatenate([ref[offset : offset + columns], ref[offset + columns :]], axis=1)
    return maps, state


def round_kernel(j, last, bits_ref, maps_ref, state_ref, other_ref, *refs):
    turn_ref, message_ref, next_state_ref, *next_maps_ref = refs
    right = pick(bits_ref, j + 1)
    columns = state_ref.shape[0]
    own, own_state = maps_ref[...], state_ref[...]
    other, other_state = open_message(other_ref, columns)
    first, second = jnp.where(right, other, own), jnp.where(right, own, other)
    maps, turn = join_maps(first, second)
    early = jnp.where(right, other_state, own_state)
    late = jnp.where(right, own_state, other_state)
    entry = early[:, :TILE]
    state = jnp.concatenate(
        [
            late[:, :TILE] + fine_dot(entry, second[:TILE], ((1,), (1,))),
            early[:, TILE:] + fine_dot(late[:, TILE:], first[:TILE]) + fine_dot(entry, turn),
        ],
        axis=1,
    )
    if last:
        message_ref[...] = last_message(pick(bits_ref, j + 2), maps, state)
    else:
        message_ref[...] = message(maps, state)
        next_maps_ref[0][...] = maps
    next_state_ref[...] = state
    turn_ref[...] = turn


def join_state(first, second, weights):
    mixed = jnp.concatenate([first[:, :TILE], second[:, TILE:]], axis=1)
    kept = jnp.concatenate([second[:, :TILE], first[:, TILE:]], axis=1)
    return kept + fine_dot(mixed, weights)


def start_kernel(
    bits_ref, parts_ref, level_ref, sibling_ref, weights_ref,
    owns_ref, states_ref, state_ref,
):
    odd = pick(bits_ref, 0)
    reps, height = parts_ref.shape[0] // 2, parts_ref.shape[2]
    own_gain, other_gain = level_ref[:height], sibling_ref[:height]
    gains = (jnp.where(odd, other_gain, own_gain), jnp.where(odd, own_gain, other_gain))
    states = []
    for c in range(2):
        own = parts_ref[c * reps]
        for r in range(1, reps):
            own = own + parts_ref[c * reps + r]
        owns_ref[c] = own
        states.append(jnp.concatenate([own[:, TILE:], -fine_dot(own, gains[c])], axis=1))
        states_ref[c] = states[c]
    state_ref[...] = join_state(states[0], states[1], weights_ref[...])


def state_kernel(j, bits_ref, own_ref, other_ref, weights_ref, *refs):
    right = pick(bits_ref, j + 1)
    own, other = own_ref[...], other_ref[...]
    state = join_state(
        jnp.where(right, other, own), jnp.where(right, own, other), weights_ref[...]
    )
    if len(refs) == 1:
        state_ref = refs[0]
    else:
        maps_ref, state_ref, message_ref = refs
        message_ref[...] = message(maps_ref[...], state)
    state_ref[...] = state


def descend_kernel(rounds, bits_ref, level_ref, sibling_ref, weights_ref, owns_ref, states_ref, *refs):
    pushes, steps = refs[:rounds], refs[rounds : 2 * rounds]
    descent_ref = refs[-1]
    odd = pick(bits_ref, 0)
    height = owns_ref.shape[2]

    def under(constant):
        return jnp.concatenate([jnp.zeros((TILE, constant.shape[1]), jnp.float32), constant], axis=0)

    row = lax.broadcasted_iota(jnp.int32, (TILE + owns_ref.shape[1], TILE), 0)
    lane = lax.broadcasted_iota(jnp.int32, (TILE + owns_ref.shape[1], TILE), 1)
    basis = jnp.where(row == lane, 1.0, 0.0)
    right = pick(bits_ref, rounds + 1)
    before, after = jnp.where(right, basis, 0.0), jnp.where(right, 0.0, basis)
    for j in reversed(range(rounds)):
        right = pick(bits_ref, j + 1)
        push = under(pushes[j][...]) + fine_dot(jnp.concatenate([before, after], axis=1), steps[j][...])
        before, after = jnp.where(right, push, before), jnp.where(right, after, push)
    own, other = level_ref[...], sibling_ref[...]
    levels = (jnp.where(odd, other, own), jnp.where(odd, own, other))
    maps = [level[TILE : 3 * TILE] for level in levels]
    entry = states_ref[0, :, :TILE]
    middle_before = under(entry) + fine_dot(before, maps[0][:TILE], ((1,), (1,)))
    middle_after = (
        under(states_ref[1, :, TILE:] + fine_dot(entry, maps[1][TILE:]))
        + fine_dot(before, weights_ref[:TILE, TILE:], ((1,), (1,)))
        + fine_dot(after, maps[1][:TILE])
    )
    ends = ((before, middle_after), (middle_before, after))
    for c in range(2):
        level = levels[c]
        forward = under(owns_ref[c]) + fine_dot(ends[c][0], level[:height], ((1,), (1,)))
        forward = jnp.concatenate(
            [forward[:, :TILE], forward[:, TILE:] - ends[c][1]], axis=1
        )
        descent_ref[:, 2 * c * TILE : (2 * c + 1) * TILE] = fine_dot(
            forward, level[height + TILE : 2 * height + TILE]
        )
        descent_ref[:, (2 * c + 1) * TILE : (2 * c + 2) * TILE] = fine_dot(
            forward, level[2 * height + TILE :]
        )


def finish_kernel(rounds, bits_ref, state_ref, other_ref, descent_ref, shares_ref):
    offset = HALF + 8
    half = other_ref[offset:]
    answered = fine_dot(state_ref[:, :TILE], unpack(other_ref[:offset]))
    push = half + jnp.where(pick(bits_ref, rounds), 0.0, answered)
    both = descent_ref[TILE:] + fine_dot(push, descent_ref[:TILE])
    reps, height = shares_ref.shape[0] // 2, shares_ref.shape[2]
    for c in range(2):
        for r in range(reps):
            shares_ref[c * reps + r] = both[:, c * height : (c + 1) * height]


def live_columns(tiles, rows, columns):
    return lax.broadcasted_iota(jnp.int32, (rows, columns), 1) < TILE * tiles


def first_kernel(
    inverse_hbm, couple_hbm, rhs_hbm, tiles_hbm, subtree_inverse_hbm, update_hbm, rows_hbm,
    level_rhs_hbm,
    level_hbm, forward_hbm, part_ref,
    inverse_ref, couple_ref, rhs_ref, tiles_ref, subtree_inverse_ref, update_ref, rows_ref,
    level_rhs_ref, sems, level_ref, forward_ref, store_sems,
):
    copies = fetch(
        sems,
        (inverse_hbm, inverse_ref),
        (couple_hbm, couple_ref),
        (rhs_hbm, rhs_ref),
        (tiles_hbm, tiles_ref),
        (subtree_inverse_hbm, subtree_inverse_ref),
        (update_hbm, update_ref),
        (rows_hbm, rows_ref),
        (level_rhs_hbm, level_rhs_ref),
    )
    height = inverse_ref.shape[0]
    copies[0].wait()
    copies[1].wait()
    gain = -fine_dot(inverse_ref[...], couple_ref[...])
    level_ref[:height] = gain
    level_ref[height : height + TILE] = -fine_dot(gain.T, gain)
    level_ref[height + TILE : 2 * height + TILE] = inverse_ref[:, :TILE]
    level_ref[2 * height + TILE :] = inverse_ref[:, TILE:]
    store_level = pltpu.make_async_copy(level_ref, level_hbm, store_sems.at[0])
    store_level.start()
    columns, sub_rows = rhs_ref.shape[1], rhs_ref.shape[0]
    copies[2].wait()
    copies[3].wait()
    live = live_columns(tiles_ref[...], columns, sub_rows)
    masked = jnp.where(live, rhs_ref[...].astype(jnp.float32).T, 0.0).astype(jnp.bfloat16)
    copies[4].wait()
    solved = dot(masked, subtree_inverse_ref[...], ((1,), (1,)))
    forward = jnp.where(live, solved, 0.0).astype(jnp.bfloat16)
    forward_ref[:columns] = forward
    copies[5].wait()
    contrib = dot(forward, update_ref[...], ((1,), (1,)))
    copies[6].wait()
    totals = []
    for s in range(level_rhs_ref.shape[0] // TILE):
        total = jnp.zeros((columns, TILE), jnp.float32)
        for t in range(rows_ref.shape[1]):
            here = rows_ref[:, t : t + 1] == s
            total = total + jnp.where(here, contrib[:, t * TILE : (t + 1) * TILE], 0.0)
        totals.append(total)
    row = lax.broadcasted_iota(jnp.int32, (MARKS, sub_rows), 0)
    lane = lax.broadcasted_iota(jnp.int32, (MARKS, sub_rows), 1)
    marks = jnp.where(row == 0, tiles_ref[...], 0)
    for t in range(rows_ref.shape[1]):
        marks = jnp.where((row == 1) & (lane == t), rows_ref[:, t : t + 1], marks)
    forward_ref[columns:] = marks.astype(jnp.float32).astype(jnp.bfloat16)
    store_forward = pltpu.make_async_copy(forward_ref, forward_hbm, store_sems.at[1])
    store_forward.start()
    copies[7].wait()
    rest = 0.25 * level_rhs_ref[...].T - jnp.concatenate(totals, axis=1)
    part_ref[...] = fine_dot(rest, inverse_ref[...], ((1,), (1,)))
    store_level.wait()
    store_forward.wait()


def subtree_backward_kernel(
    solution_ref, forward_ref, subtree_inverse_ref, update_ref, level_ref, final_ref
):
    columns, sub_rows = solution_ref.shape[0], forward_ref.shape[1]
    marks = forward_ref[columns:].astype(jnp.float32).astype(jnp.int32)
    live = live_columns(marks[:1, :1], columns, sub_rows)
    level_ref[...] = solution_ref[...].T
    picked = []
    for t in range(update_ref.shape[0] // TILE):
        tile = solution_ref[:, :TILE]
        for s in range(1, solution_ref.shape[1] // TILE):
            here = marks[1:2, t : t + 1] == s
            tile = jnp.where(here, solution_ref[:, s * TILE : (s + 1) * TILE], tile)
        picked.append(tile.astype(jnp.bfloat16))
    pulled = dot(jnp.concatenate(picked, axis=1), update_ref[...])
    residue = forward_ref[:columns].astype(jnp.float32) - jnp.where(live, pulled, 0.0)
    final = dot(residue.astype(jnp.bfloat16), subtree_inverse_ref[...])
    final_ref[...] = jnp.where(live, final, 0.0).T


def local_call(
    kernel, out_shape, *operands, fetched=(), later=(), weight=0, limit=8 * 2**20, stored=0
):
    vmem = pl.BlockSpec(memory_space=pltpu.VMEM)
    scratch = [pltpu.VMEM(part.shape, part.dtype) for part in fetched]
    if fetched:
        scratch.append(pltpu.SemaphoreType.DMA((len(fetched),)))
    if stored:
        scratch += [pltpu.VMEM(part.shape, part.dtype) for part in out_shape[:stored]]
        scratch.append(pltpu.SemaphoreType.DMA((stored,)))
    return pl.pallas_call(
        kernel,
        out_shape=out_shape,
        in_specs=[vmem] * len(operands)
        + [pl.BlockSpec(memory_space=pltpu.HBM)] * len(fetched)
        + [pl.BlockSpec(memory_space=pl.ANY)] * len(later),
        out_specs=[pl.BlockSpec(memory_space=pltpu.HBM)] * stored
        + [vmem] * (len(out_shape) - stored),
        scratch_shapes=scratch,
        cost_estimate=pl.CostEstimate(
            flops=weight * 10**9, bytes_accessed=weight * 2**20, transcendentals=0
        ),
        compiler_params=pltpu.CompilerParams(vmem_limit_bytes=limit),
    )(*operands, *fetched, *later)


def f32(*shape):
    return jax.ShapeDtypeStruct(shape, jnp.float32)


def shards(
    sub_inverse, sub_rhs, sub_tiles, update, update_rows, level_inverse, coupling, level_rhs
):
    count, place = lax.axis_size("pair"), lax.axis_index("pair")
    group = ("core", "rep")
    members = lax.axis_size(group)
    subtree_inverse, rhs_sub, block, rows = sub_inverse[0, 0], sub_rhs[0, 0], update[0, 0], update_rows[0]
    inverse, couple, rhs_level = level_inverse[0], coupling[0], level_rhs[0]
    sub_rows, width, height = subtree_inverse.shape[0], rhs_level.shape[1], inverse.shape[0]
    rounds = len(SWAP)
    spot = 2 * place + lax.axis_index("core")
    bits = (spot >> lax.broadcasted_iota(jnp.int32, (8, 128), 0)) & 1
    level, forward_sub, part = local_call(
        first_kernel,
        [
            f32(3 * height + TILE, TILE),
            jax.ShapeDtypeStruct((width + MARKS, sub_rows), jnp.bfloat16),
            f32(width, height),
        ],
        fetched=(inverse, couple, rhs_sub, sub_tiles, subtree_inverse, block, rows, rhs_level),
        limit=66 * 10**6, stored=2,
    )
    sibling = lax.ppermute(level, "core", [(0, 1), (1, 0)])
    maps, pair_weights = local_call(
        pair_kernel, [f32(2 * TILE, TILE), f32(2 * TILE, 2 * TILE)], bits, level, sibling
    )
    columns = width // members
    parts = lax.all_to_all(part.reshape(members, columns, height), group, 0, 0)
    pushes, steps = [], []
    square = 2 * TILE

    def set_aside(j, maps, state, turn, *others):
        step, push = local_call(
            functools.partial(side_kernel, j),
            [f32(square, TILE), f32(columns, TILE)],
            bits, maps, state, turn, *others, weight=SIDE_WEIGHT,
        )
        steps.append(step)
        pushes.append(push)

    def advance_maps(j, maps, *later):
        other = swap(maps, j, count)
        joined, weights = local_call(
            functools.partial(maps_kernel, j, len(later)),
            [f32(square, TILE), f32(square, square)],
            bits, maps, other, later=later, weight=MAPS_WEIGHT[j],
        )
        return maps, other, joined, weights

    own_maps, other_maps, maps, weights = advance_maps(0, maps, parts)
    owns, states, state = local_call(
        start_kernel,
        [f32(2, columns, height), f32(2, columns, square), f32(columns, square)],
        bits, parts, level, sibling, pair_weights,
    )
    whole = TILE + HALF + 8 + 2 * columns
    for j in range(APART):
        other = swap(state, j, count)
        shapes = [f32(columns, square)]
        operands = [bits, state, other, weights]
        aside = (j, own_maps, state, weights, other_maps, other)
        if j + 1 < APART:
            own_maps, other_maps, maps, weights = advance_maps(j + 1, maps, state)
        else:
            operands.append(maps)
            shapes.append(f32(whole, TILE))
        state, *packed = local_call(
            functools.partial(state_kernel, j), shapes, *operands, weight=STATE_WEIGHT[j]
        )
        set_aside(*aside)
    packed = packed[0]
    for j in range(APART, rounds - 1):
        last = j == rounds - 2
        shapes = [
            f32(TILE, TILE),
            f32(HALF + 8 + columns if last else whole, TILE),
            f32(columns, square),
        ]
        other = swap(packed, j, count)
        aside = (j, maps, state)
        turn, packed, state, *rest = local_call(
            functools.partial(round_kernel, j, last),
            shapes if last else shapes + [f32(square, TILE)],
            bits, maps, state, other,
        )
        set_aside(*aside, turn, other)
        maps = None if last else rest[0]
    got = swap(packed, rounds - 1, count)
    (descent,) = local_call(
        functools.partial(descend_kernel, rounds - 1),
        [f32(TILE + columns, 2 * height)],
        bits, level, sibling, pair_weights, owns, states, *pushes, *steps,
    )
    (shares,) = local_call(
        functools.partial(finish_kernel, rounds),
        [f32(members, columns, height)],
        bits, state, got, descent,
    )
    spread = lax.all_to_all(shares, group, 0, 0)
    solution, final = local_call(
        subtree_backward_kernel,
        [f32(height, width), f32(sub_rows, width)],
        spread.reshape(width, -1), forward_sub, subtree_inverse, block,
    )
    return (solution[None], final[None, None])


def solution(mesh):
    chain, reps = mesh.devices.shape
    split = Mesh(mesh.devices.reshape(chain // 2, 2, reps), ("pair", "core", "rep"))
    both = ("pair", "core")
    return jax.shard_map(
        shards,
        mesh=split,
        in_specs=(
            P(both, "rep", None, None),
            P(both, "rep", None, None),
            P(both, "rep"),
            P(both, "rep", None, None),
            P(both, "rep", None),
            P(both, None, None),
            P(both, None, None),
            P(both, None, None),
        ),
        out_specs=(P(both, None, None), P(both, "rep", None, None)),
        check_vma=False,
    )
```

```python
import functools

import jax
import jax.numpy as jnp
from jax import lax
from jax.experimental import pallas as pl
from jax.experimental.pallas import tpu as pltpu
from jax.sharding import Mesh, PartitionSpec as P

TILE = 128
HALF = TILE // 2
MARKS = 16
SWAP = (1, 3, 4, 8, 16, 48)


APART = 1
MAPS_WEIGHT = (3, 10)
STATE_WEIGHT = (30, 10)
SIDE_WEIGHT = 1


def dot(a, b, dims=((1,), (0,))):
    return lax.dot_general(a, b, (dims, ((), ())), preferred_element_type=jnp.float32)


def halves(value):
    high = value.astype(jnp.bfloat16)
    return high, (value - high.astype(jnp.float32)).astype(jnp.bfloat16)


def fine_dot(a, b, dims=((1,), (0,))):
    (a_high, a_low), (b_high, b_low) = halves(a), halves(b)
    small = dot(a_high, b_low, dims) + dot(a_low, b_high, dims)
    return small + dot(a_high, b_high, dims)


def swap(value, j, count):
    return lax.ppermute(value, "pair", [(n, n ^ SWAP[j]) for n in range(count)])


def pick(bits_ref, at):
    return bits_ref[at : at + 1, :1] == 1


def fetch(sems, *pairs):
    copies = [
        pltpu.make_async_copy(source, target, sems.at[i])
        for i, (source, target) in enumerate(pairs)
    ]
    for copy in copies:
        copy.start()
    return copies


def corners():
    row = lax.broadcasted_iota(jnp.int32, (HALF, TILE), 0)
    lane = lax.broadcasted_iota(jnp.int32, (HALF, TILE), 1)
    return row, lane


def pack(square):
    row, lane = corners()
    top, bottom = square[:HALF], square[HALF:]
    body = jnp.where((lane >= HALF) & (row > lane - HALF), pltpu.roll(top, HALF, 1), bottom)
    diagonal = jnp.sum(jnp.where(row == lane, top, 0.0), axis=0, keepdims=True)
    return jnp.concatenate([body, jnp.broadcast_to(diagonal, (8, TILE))], axis=0)


def unpack(packed):
    row, lane = corners()
    body, diagonal = packed[:HALF], packed[HALF : HALF + 1]
    first = jnp.where((lane < HALF) & (row > lane), pltpu.roll(body, HALF, 1), 0.0)
    first = jnp.where(row == lane, 0.5 * diagonal, first)
    last = jnp.where((lane < HALF) | (row < lane - HALF), body, 0.0)
    last = jnp.where(row == lane - HALF, 0.5 * body, last)
    half = jnp.concatenate([first, last], axis=0)
    return half + half.T


def join_maps(first, second):
    early = first[:TILE]
    product = fine_dot(second, early)
    turn = product[TILE:]
    answer = first[TILE:] + fine_dot(early.T, turn)
    return jnp.concatenate([product[:TILE], answer], axis=0), turn


def fill_weights(first, second, turn, weights_ref):
    weights_ref[:TILE, :TILE] = second[:TILE].T
    weights_ref[:TILE, TILE:] = turn
    weights_ref[TILE:, :TILE] = jnp.zeros_like(turn)
    weights_ref[TILE:, TILE:] = first[:TILE]


def pair_kernel(bits_ref, level_ref, sibling_ref, maps_ref, weights_ref):
    odd = pick(bits_ref, 0)
    own, other = level_ref[TILE : 3 * TILE], sibling_ref[TILE : 3 * TILE]
    first, second = jnp.where(odd, other, own), jnp.where(odd, own, other)
    maps_ref[...], turn = join_maps(first, second)
    fill_weights(first, second, turn, weights_ref)


def maps_kernel(j, later, bits_ref, own_ref, other_ref, *refs):
    maps_ref, weights_ref = refs[later:]
    right = pick(bits_ref, j + 1)
    own, other = own_ref[...], other_ref[...]
    first, second = jnp.where(right, other, own), jnp.where(right, own, other)
    maps_ref[...], turn = join_maps(first, second)
    fill_weights(first, second, turn, weights_ref)


def message(maps, state):
    parts = [maps[:TILE], pack(maps[TILE:]), state[:, :TILE], state[:, TILE:]]
    return jnp.concatenate(parts, axis=0)


def last_message(right, maps, state):
    half = jnp.where(right, state[:, TILE:], state[:, :TILE])
    return jnp.concatenate([pack(maps[TILE:]), half], axis=0)


def side_kernel(j, bits_ref, own_ref, state_ref, turn_ref, *refs):
    *others, step_ref, push_ref = refs
    right = pick(bits_ref, j + 1)
    columns, square = state_ref.shape
    if len(others) == 2:
        other, other_state = others[0][...], others[1][...]
        turn = turn_ref[:TILE, TILE:]
    else:
        other, other_state = open_message(others[0], columns)
        turn = turn_ref[...]
    own = own_ref[...]
    step_ref[:TILE] = jnp.where(right, other[:TILE], turn).T
    step_ref[TILE:] = jnp.where(right, 0.0, other[:TILE])
    push_ref[...] = jnp.where(
        right,
        other_state[:, :TILE],
        other_state[:, TILE:] + fine_dot(state_ref[:, :TILE], other[TILE:]),
    )


def open_message(ref, columns):
    offset = TILE + HALF + 8
    maps = jnp.concatenate([ref[:TILE], unpack(ref[TILE:offset])], axis=0)
    state = jnp.concatenate([ref[offset : offset + columns], ref[offset + columns :]], axis=1)
    return maps, state


def round_kernel(j, last, bits_ref, maps_ref, state_ref, other_ref, *refs):
    turn_ref, message_ref, next_state_ref, *next_maps_ref = refs
    right = pick(bits_ref, j + 1)
    columns = state_ref.shape[0]
    own, own_state = maps_ref[...], state_ref[...]
    other, other_state = open_message(other_ref, columns)
    first, second = jnp.where(right, other, own), jnp.where(right, own, other)
    maps, turn = join_maps(first, second)
    early = jnp.where(right, other_state, own_state)
    late = jnp.where(right, own_state, other_state)
    entry = early[:, :TILE]
    state = jnp.concatenate(
        [
            late[:, :TILE] + fine_dot(entry, second[:TILE], ((1,), (1,))),
            early[:, TILE:] + fine_dot(late[:, TILE:], first[:TILE]) + fine_dot(entry, turn),
        ],
        axis=1,
    )
    if last:
        message_ref[...] = last_message(pick(bits_ref, j + 2), maps, state)
    else:
        message_ref[...] = message(maps, state)
        next_maps_ref[0][...] = maps
    next_state_ref[...] = state
    turn_ref[...] = turn


def join_state(first, second, weights):
    mixed = jnp.concatenate([first[:, :TILE], second[:, TILE:]], axis=1)
    kept = jnp.concatenate([second[:, :TILE], first[:, TILE:]], axis=1)
    return kept + fine_dot(mixed, weights)


def start_kernel(
    bits_ref, parts_ref, level_ref, sibling_ref, weights_ref,
    owns_ref, states_ref, state_ref,
):
    odd = pick(bits_ref, 0)
    reps, height = parts_ref.shape[0] // 2, parts_ref.shape[2]
    own_gain, other_gain = level_ref[:height], sibling_ref[:height]
    gains = (jnp.where(odd, other_gain, own_gain), jnp.where(odd, own_gain, other_gain))
    states = []
    for c in range(2):
        own = parts_ref[c * reps]
        for r in range(1, reps):
            own = own + parts_ref[c * reps + r]
        owns_ref[c] = own
        states.append(jnp.concatenate([own[:, TILE:], -fine_dot(own, gains[c])], axis=1))
        states_ref[c] = states[c]
    state_ref[...] = join_state(states[0], states[1], weights_ref[...])


def state_kernel(j, bits_ref, own_ref, other_ref, weights_ref, *refs):
    right = pick(bits_ref, j + 1)
    own, other = own_ref[...], other_ref[...]
    state = join_state(
        jnp.where(right, other, own), jnp.where(right, own, other), weights_ref[...]
    )
    if len(refs) == 1:
        state_ref = refs[0]
    else:
        maps_ref, state_ref, message_ref = refs
        message_ref[...] = message(maps_ref[...], state)
    state_ref[...] = state


def descend_kernel(rounds, bits_ref, level_ref, sibling_ref, weights_ref, owns_ref, states_ref, *refs):
    pushes, steps = refs[:rounds], refs[rounds : 2 * rounds]
    descent_ref = refs[-1]
    odd = pick(bits_ref, 0)
    height = owns_ref.shape[2]

    def under(constant):
        return jnp.concatenate([jnp.zeros((TILE, constant.shape[1]), jnp.float32), constant], axis=0)

    row = lax.broadcasted_iota(jnp.int32, (TILE + owns_ref.shape[1], TILE), 0)
    lane = lax.broadcasted_iota(jnp.int32, (TILE + owns_ref.shape[1], TILE), 1)
    basis = jnp.where(row == lane, 1.0, 0.0)
    right = pick(bits_ref, rounds + 1)
    before, after = jnp.where(right, basis, 0.0), jnp.where(right, 0.0, basis)
    for j in reversed(range(rounds)):
        right = pick(bits_ref, j + 1)
        push = under(pushes[j][...]) + fine_dot(jnp.concatenate([before, after], axis=1), steps[j][...])
        before, after = jnp.where(right, push, before), jnp.where(right, after, push)
    own, other = level_ref[...], sibling_ref[...]
    levels = (jnp.where(odd, other, own), jnp.where(odd, own, other))
    maps = [level[TILE : 3 * TILE] for level in levels]
    entry = states_ref[0, :, :TILE]
    middle_before = under(entry) + fine_dot(before, maps[0][:TILE], ((1,), (1,)))
    middle_after = (
        under(states_ref[1, :, TILE:] + fine_dot(entry, maps[1][TILE:]))
        + fine_dot(before, weights_ref[:TILE, TILE:], ((1,), (1,)))
        + fine_dot(after, maps[1][:TILE])
    )
    ends = ((before, middle_after), (middle_before, after))
    for c in range(2):
        level = levels[c]
        forward = under(owns_ref[c]) + fine_dot(ends[c][0], level[:height], ((1,), (1,)))
        forward = jnp.concatenate(
            [forward[:, :TILE], forward[:, TILE:] - ends[c][1]], axis=1
        )
        descent_ref[:, 2 * c * TILE : (2 * c + 1) * TILE] = fine_dot(
            forward, level[height + TILE : 2 * height + TILE]
        )
        descent_ref[:, (2 * c + 1) * TILE : (2 * c + 2) * TILE] = fine_dot(
            forward, level[2 * height + TILE :]
        )


def finish_kernel(rounds, bits_ref, state_ref, other_ref, descent_ref, shares_ref):
    offset = HALF + 8
    half = other_ref[offset:]
    answered = fine_dot(state_ref[:, :TILE], unpack(other_ref[:offset]))
    push = half + jnp.where(pick(bits_ref, rounds), 0.0, answered)
    both = descent_ref[TILE:] + fine_dot(push, descent_ref[:TILE])
    reps, height = shares_ref.shape[0] // 2, shares_ref.shape[2]
    for c in range(2):
        for r in range(reps):
            shares_ref[c * reps + r] = both[:, c * height : (c + 1) * height]


def live_columns(tiles, rows, columns):
    return lax.broadcasted_iota(jnp.int32, (rows, columns), 1) < TILE * tiles


def first_kernel(
    inverse_hbm, couple_hbm, rhs_hbm, tiles_hbm, subtree_inverse_hbm, update_hbm, rows_hbm,
    level_rhs_hbm,
    level_hbm, forward_hbm, part_ref,
    inverse_ref, couple_ref, rhs_ref, tiles_ref, subtree_inverse_ref, update_ref, rows_ref,
    level_rhs_ref, sems, level_ref, forward_ref, store_sems,
):
    copies = fetch(
        sems,
        (inverse_hbm, inverse_ref),
        (couple_hbm, couple_ref),
        (rhs_hbm, rhs_ref),
        (tiles_hbm, tiles_ref),
        (subtree_inverse_hbm, subtree_inverse_ref),
        (update_hbm, update_ref),
        (rows_hbm, rows_ref),
        (level_rhs_hbm, level_rhs_ref),
    )
    height = inverse_ref.shape[0]
    copies[0].wait()
    copies[1].wait()
    gain = -fine_dot(inverse_ref[...], couple_ref[...])
    level_ref[:height] = gain
    level_ref[height : height + TILE] = -fine_dot(gain.T, gain)
    level_ref[height + TILE : 2 * height + TILE] = inverse_ref[:, :TILE]
    level_ref[2 * height + TILE :] = inverse_ref[:, TILE:]
    store_level = pltpu.make_async_copy(level_ref, level_hbm, store_sems.at[0])
    store_level.start()
    columns, sub_rows = rhs_ref.shape[1], rhs_ref.shape[0]
    copies[2].wait()
    copies[3].wait()
    live = live_columns(tiles_ref[...], columns, sub_rows)
    masked = jnp.where(live, rhs_ref[...].astype(jnp.float32).T, 0.0).astype(jnp.bfloat16)
    copies[4].wait()
    solved = dot(masked, subtree_inverse_ref[...], ((1,), (1,)))
    forward = jnp.where(live, solved, 0.0).astype(jnp.bfloat16)
    forward_ref[:columns] = forward
    copies[5].wait()
    contrib = dot(forward, update_ref[...], ((1,), (1,)))
    copies[6].wait()
    totals = []
    for s in range(level_rhs_ref.shape[0] // TILE):
        total = jnp.zeros((columns, TILE), jnp.float32)
        for t in range(rows_ref.shape[1]):
            here = rows_ref[:, t : t + 1] == s
            total = total + jnp.where(here, contrib[:, t * TILE : (t + 1) * TILE], 0.0)
        totals.append(total)
    row = lax.broadcasted_iota(jnp.int32, (MARKS, sub_rows), 0)
    lane = lax.broadcasted_iota(jnp.int32, (MARKS, sub_rows), 1)
    marks = jnp.where(row == 0, tiles_ref[...], 0)
    for t in range(rows_ref.shape[1]):
        marks = jnp.where((row == 1) & (lane == t), rows_ref[:, t : t + 1], marks)
    forward_ref[columns:] = marks.astype(jnp.float32).astype(jnp.bfloat16)
    store_forward = pltpu.make_async_copy(forward_ref, forward_hbm, store_sems.at[1])
    store_forward.start()
    copies[7].wait()
    rest = 0.25 * level_rhs_ref[...].T - jnp.concatenate(totals, axis=1)
    part_ref[...] = fine_dot(rest, inverse_ref[...], ((1,), (1,)))
    store_level.wait()
    store_forward.wait()


def subtree_backward_kernel(
    solution_ref, forward_ref, subtree_inverse_ref, update_ref, level_ref, final_ref
):
    columns, sub_rows = solution_ref.shape[0], forward_ref.shape[1]
    marks = forward_ref[columns:].astype(jnp.float32).astype(jnp.int32)
    live = live_columns(marks[:1, :1], columns, sub_rows)
    level_ref[...] = solution_ref[...].T
    picked = []
    for t in range(update_ref.shape[0] // TILE):
        tile = solution_ref[:, :TILE]
        for s in range(1, solution_ref.shape[1] // TILE):
            here = marks[1:2, t : t + 1] == s
            tile = jnp.where(here, solution_ref[:, s * TILE : (s + 1) * TILE], tile)
        picked.append(tile.astype(jnp.bfloat16))
    pulled = dot(jnp.concatenate(picked, axis=1), update_ref[...])
    residue = forward_ref[:columns].astype(jnp.float32) - jnp.where(live, pulled, 0.0)
    final = dot(residue.astype(jnp.bfloat16), subtree_inverse_ref[...])
    final_ref[...] = jnp.where(live, final, 0.0).T


def local_call(
    kernel, out_shape, *operands, fetched=(), later=(), weight=0, limit=8 * 2**20, stored=0
):
    vmem = pl.BlockSpec(memory_space=pltpu.VMEM)
    scratch = [pltpu.VMEM(part.shape, part.dtype) for part in fetched]
    if fetched:
        scratch.append(pltpu.SemaphoreType.DMA((len(fetched),)))
    if stored:
        scratch += [pltpu.VMEM(part.shape, part.dtype) for part in out_shape[:stored]]
        scratch.append(pltpu.SemaphoreType.DMA((stored,)))
    return pl.pallas_call(
        kernel,
        out_shape=out_shape,
        in_specs=[vmem] * len(operands)
        + [pl.BlockSpec(memory_space=pltpu.HBM)] * len(fetched)
        + [pl.BlockSpec(memory_space=pl.ANY)] * len(later),
        out_specs=[pl.BlockSpec(memory_space=pltpu.HBM)] * stored
        + [vmem] * (len(out_shape) - stored),
        scratch_shapes=scratch,
        cost_estimate=pl.CostEstimate(
            flops=weight * 10**9, bytes_accessed=weight * 2**20, transcendentals=0
        ),
        compiler_params=pltpu.CompilerParams(vmem_limit_bytes=limit),
    )(*operands, *fetched, *later)


def f32(*shape):
    return jax.ShapeDtypeStruct(shape, jnp.float32)


def shards(
    sub_inverse, sub_rhs, sub_tiles, update, update_rows, level_inverse, coupling, level_rhs
):
    count, place = lax.axis_size("pair"), lax.axis_index("pair")
    group = ("core", "rep")
    members = lax.axis_size(group)
    subtree_inverse, rhs_sub, block, rows = sub_inverse[0, 0], sub_rhs[0, 0], update[0, 0], update_rows[0]
    inverse, couple, rhs_level = level_inverse[0], coupling[0], level_rhs[0]
    sub_rows, width, height = subtree_inverse.shape[0], rhs_level.shape[1], inverse.shape[0]
    rounds = len(SWAP)
    spot = 2 * place + lax.axis_index("core")
    bits = (spot >> lax.broadcasted_iota(jnp.int32, (8, 128), 0)) & 1
    level, forward_sub, part = local_call(
        first_kernel,
        [
            f32(3 * height + TILE, TILE),
            jax.ShapeDtypeStruct((width + MARKS, sub_rows), jnp.bfloat16),
            f32(width, height),
        ],
        fetched=(inverse, couple, rhs_sub, sub_tiles, subtree_inverse, block, rows, rhs_level),
        limit=66 * 10**6, stored=2,
    )
    sibling = lax.ppermute(level, "core", [(0, 1), (1, 0)])
    maps, pair_weights = local_call(
        pair_kernel, [f32(2 * TILE, TILE), f32(2 * TILE, 2 * TILE)], bits, level, sibling
    )
    columns = width // members
    parts = lax.all_to_all(part.reshape(members, columns, height), group, 0, 0)
    pushes, steps = [], []
    square = 2 * TILE

    def set_aside(j, maps, state, turn, *others):
        step, push = local_call(
            functools.partial(side_kernel, j),
            [f32(square, TILE), f32(columns, TILE)],
            bits, maps, state, turn, *others, weight=SIDE_WEIGHT,
        )
        steps.append(step)
        pushes.append(push)

    def advance_maps(j, maps, *later):
        other = swap(maps, j, count)
        joined, weights = local_call(
            functools.partial(maps_kernel, j, len(later)),
            [f32(square, TILE), f32(square, square)],
            bits, maps, other, later=later, weight=MAPS_WEIGHT[j],
        )
        return maps, other, joined, weights

    own_maps, other_maps, maps, weights = advance_maps(0, maps, parts)
    owns, states, state = local_call(
        start_kernel,
        [f32(2, columns, height), f32(2, columns, square), f32(columns, square)],
        bits, parts, level, sibling, pair_weights,
    )
    whole = TILE + HALF + 8 + 2 * columns
    for j in range(APART):
        other = swap(state, j, count)
        shapes = [f32(columns, square)]
        operands = [bits, state, other, weights]
        aside = (j, own_maps, state, weights, other_maps, other)
        if j + 1 < APART:
            own_maps, other_maps, maps, weights = advance_maps(j + 1, maps, state)
        else:
            operands.append(maps)
            shapes.append(f32(whole, TILE))
        state, *packed = local_call(
            functools.partial(state_kernel, j), shapes, *operands, weight=STATE_WEIGHT[j]
        )
        set_aside(*aside)
    packed = packed[0]
    for j in range(APART, rounds - 1):
        last = j == rounds - 2
        shapes = [
            f32(TILE, TILE),
            f32(HALF + 8 + columns if last else whole, TILE),
            f32(columns, square),
        ]
        other = swap(packed, j, count)
        aside = (j, maps, state)
        turn, packed, state, *rest = local_call(
            functools.partial(round_kernel, j, last),
            shapes if last else shapes + [f32(square, TILE)],
            bits, maps, state, other,
        )
        set_aside(*aside, turn, other)
        maps = None if last else rest[0]
    got = swap(packed, rounds - 1, count)
    (descent,) = local_call(
        functools.partial(descend_kernel, rounds - 1),
        [f32(TILE + columns, 2 * height)],
        bits, level, sibling, pair_weights, owns, states, *pushes, *steps,
    )
    (shares,) = local_call(
        functools.partial(finish_kernel, rounds),
        [f32(members, columns, height)],
        bits, state, got, descent,
    )
    spread = lax.all_to_all(shares, group, 0, 0)
    solution, final = local_call(
        subtree_backward_kernel,
        [f32(height, width), f32(sub_rows, width)],
        spread.reshape(width, -1), forward_sub, subtree_inverse, block,
    )
    return (solution[None], final[None, None])


def solution(mesh):
    chain, reps = mesh.devices.shape
    split = Mesh(mesh.devices.reshape(chain // 2, 2, reps), ("pair", "core", "rep"))
    both = ("pair", "core")
    return jax.shard_map(
        shards,
        mesh=split,
        in_specs=(
            P(both, "rep", None, None),
            P(both, "rep", None, None),
            P(both, "rep"),
            P(both, "rep", None, None),
            P(both, "rep", None),
            P(both, None, None),
            P(both, None, None),
            P(both, None, None),
        ),
        out_specs=(P(both, None, None), P(both, "rep", None, None)),
        check_vma=False,
    )
```
